128 devices in a mesh: ctx: 16 (over x, z), head: 8 (over y, core).
Axes of the slice: x: 4, y: 4, z: 4, core: 2. Of those that a mesh axis runs over, the one named last changes fastest.
Arguments:
- activations: bfloat16 [32768, 2304], P('ctx'), may hold values from -6 to 6
- norm_gain: float32 [2304], replicated, may hold values from 0.1 to 1.9
- qkv_weight: bfloat16 [3, 2304, 2048], P(None, None, 'head'), may hold values from -0.125 to 0.125
- conv_weight: bfloat16 [3, 4, 2048], P(None, None, 'head'), may hold values from -3 to 3
- gate_down_matrix: bfloat16 [2304, 128], replicated, may hold values from -0.125 to 0.125
- gate_up: bfloat16 [128, 2048], P(None, 'head'), may hold values from -0.5 to 0.5
- log_forget_gates: float32 [16, 32768, 128], P('head', 'ctx'), may hold values from -0.8 to 0
- step_size: float32 [16, 32768], P('head', 'ctx'), may hold values from 0.02 to 0.1
- out_gain: float32 [2048], P('head'), may hold values from 0.1 to 1.9
- out_weight: bfloat16 [2048, 2304], P('head'), may hold values from -0.1875 to 0.1875
Outputs:
- mixed: bfloat16 [32768, 2304], P('ctx', 'head')
The draws below stay inside these ranges and needn't reach their ends.
All inputs are finite; a program needn't handle non-finite values.
Results may differ from the reference program's by a relative error of at most 0.014.
Values may be sent and summed in bfloat16 or wider, within the bound.
No kernel may reach another device: no remote copies, remote signals or barrier semaphores. Data moves between devices by JAX's collectives and lax.ppermute only.
A program may use at most 128 MiB of HBM per device.

```python
import math
import jax
import jax.numpy as jnp
from jax import lax

D = 2304
DK = 128
RANK = 128
KERNEL = 4
TOK_DEV = 2048
HEADS = 16
TOKENS = 32768


def draw_log_forget_gates(key, part):
    key = jax.random.fold_in(key, 11)
    keys = jax.random.split(key, 7)
    fast_share = 0.25
    rough_guess = jnp.exp(jax.random.uniform(keys[3], (HEADS, TOKENS, DK), jnp.float32, math.log(0.5), math.log(1.5)))
    fast = jax.random.uniform(keys[0], (HEADS, 1, DK), jnp.float32) < fast_share
    fast_rate = jnp.exp(jax.random.uniform(keys[1], (HEADS, 1, DK), jnp.float32, math.log(1.0 / 50.0), math.log(1.0 / 30.0)))
    slow_rate = jnp.exp(jax.random.uniform(keys[2], (HEADS, 1, DK), jnp.float32, math.log(0.2), 0.0)) / TOKENS
    update_pace = jnp.where(fast, fast_rate, slow_rate)
    shrink_factor = jnp.exp(jax.random.uniform(keys[4], (HEADS, TOKENS // TOK_DEV, 1), jnp.float32, math.log(0.7), math.log(1.4)))
    shrink_factor = jnp.repeat(shrink_factor, TOK_DEV, axis=1)
    places = jax.random.randint(keys[5], (HEADS, 4), 0, TOKENS)
    aligned_indices = jnp.any(jnp.arange(TOKENS)[None, :, None] == places[:, None, :], axis=-1)
    nesting_level = jax.random.uniform(keys[6], (HEADS, 1), jnp.float32, math.log(0.5), math.log(0.8))
    segment_extent = jnp.where(aligned_indices, nesting_level, 0.0)[:, :, None]
    return -update_pace * rough_guess * shrink_factor + segment_extent


def draw_step_size(key, part):
    key = jax.random.fold_in(key, 12)
    return jnp.exp(jax.random.uniform(key, (HEADS, TOKENS), jnp.float32, math.log(0.02), math.log(0.1)))


def with_spikes(entries, rng, source, target, parts, factor):
    owner, partner = [(jnp.arange(entries.shape[axis_at]) // (entries.shape[axis_at] // parts)).reshape([-1 if axis == axis_at else 1 for axis in range(entries.ndim)]) for axis_at in (source, target)]
    chosen = jax.random.permutation(rng, parts)[partner]
    strong = (owner == chosen) | (owner == (partner + parts // 2) % parts)
    return jnp.where(strong, factor * entries, entries)


def block_levels(key, dims, cuts, smallest, top_value):
    loudness = 1.0
    for axis_at, parts in cuts:
        steps = jax.random.uniform(jax.random.fold_in(jax.random.fold_in(key, 6), axis_at), (parts,), jnp.float32, smallest / len(cuts), top_value / len(cuts))
        loudness = loudness * jnp.repeat(jnp.exp(steps), dims[axis_at] // parts).reshape((-1,) + (1,) * (len(dims) - 1 - axis_at))
    return loudness


def centred(stream_key, extent, deviation, bound, shards=(), dtype=jnp.bfloat16):
    factor_of = block_levels(stream_key, extent, shards, -0.22, 0.18) if shards else 1.0
    array = jax.random.normal(stream_key, extent, jnp.float32) * deviation * factor_of
    return jnp.minimum(jnp.maximum(array, -bound), bound).astype(dtype)


def noise_with(stream_key, dims, width, bound, cuts, heavy, kind=jnp.bfloat16):
    drawn = width * jax.random.normal(stream_key, dims, jnp.float32)
    if cuts:
        drawn = drawn * block_levels(stream_key, dims, cuts, -0.22, 0.18)
    return jnp.clip(with_spikes(drawn, jax.random.fold_in(stream_key, 3), *heavy), -bound, bound).astype(kind)


def setup_inputs(seed: int = 0) -> dict:
    arg_keys = jax.random.split(jax.random.key(seed), 11)
    return {
        "activations": centred(arg_keys[0], (TOKENS, D), 1.0, 6.0, ((0, 16),)),
        "norm_gain": jnp.clip(1.0 + 0.18 * jax.random.normal(arg_keys[1], (D,), jnp.float32), 0.1, 1.9),
        "qkv_weight": centred(arg_keys[2], (3, D, HEADS * DK), D ** -0.5, 0.125, ((2, 8),)),
        "conv_weight": centred(arg_keys[3], (3, KERNEL, HEADS * DK), 0.5, 3.0, ((2, 8),)),
        "gate_down_matrix": centred(arg_keys[4], (D, RANK), D ** -0.5, 0.125),
        "gate_up": centred(arg_keys[5], (RANK, HEADS * DK), RANK ** -0.5, 0.5, ((1, 8),)),
        "log_forget_gates": draw_log_forget_gates(jax.random.fold_in(arg_keys[10], 71), 0),
        "step_size": draw_step_size(jax.random.fold_in(arg_keys[10], 71), 0),
        "out_gain": jnp.clip(1.0 + 0.18 * jax.random.normal(arg_keys[8], (HEADS * DK,), jnp.float32), 0.1, 1.9),
        "out_weight": noise_with(arg_keys[9], (HEADS * DK, D), (HEADS * DK) ** -0.5, 0.1875, ((0, 8),), (0, 1, 8, 2.0)),
    }


def unit_rows(field, eps):
    return field * lax.rsqrt(lax.optimization_barrier(jnp.sum(field * field, axis=-1, keepdims=True)) + eps)

def reference(activations, norm_gain, qkv_weight, conv_weight, gate_down_matrix, gate_up, log_forget_gates, step_size, out_gain, out_weight):
    highest = lax.Precision.HIGHEST
    wide = activations.astype(jnp.float32)
    normed = (wide * lax.rsqrt(lax.optimization_barrier(jnp.mean(wide * wide, axis=-1, keepdims=True)) + 1e-06) * norm_gain).astype(jnp.bfloat16)
    projected = jnp.stack([jnp.dot(normed, qkv_weight[i], preferred_element_type=jnp.float32) for i in range(3)]).astype(jnp.bfloat16)
    padded = jnp.concatenate([jnp.zeros((3, KERNEL - 1, HEADS * DK), jnp.float32), projected.astype(jnp.float32)], axis=1)
    summed = jnp.zeros((3, TOKENS, HEADS * DK), jnp.float32)
    for j in range(KERNEL):
        summed = summed + conv_weight[:, j][:, None, :].astype(jnp.float32) * padded[:, j:j + TOKENS]
    convolved = jax.nn.silu(summed)
    query = unit_rows(convolved[0].reshape(TOKENS, HEADS, DK), 1e-06) / jnp.sqrt(jnp.float32(DK))
    key = unit_rows(convolved[1].reshape(TOKENS, HEADS, DK), 1e-06)
    value = convolved[2].reshape(TOKENS, HEADS, DK)

    def advance(state, inputs):
        q_row, k_row, v_row, g_row, b_row = inputs
        state = state * jnp.exp(g_row)[:, :, None]
        recalled = jnp.einsum('hc,hcj->hj', k_row, state, precision=highest)
        state = state + b_row[:, None, None] * k_row[:, :, None] * (v_row - recalled)[:, None, :]
        return (state, jnp.einsum('hc,hcj->hj', q_row, state, precision=highest))
    start = jnp.zeros((HEADS, DK, DK), jnp.float32)
    inputs = (query, key, value, jnp.transpose(log_forget_gates, (1, 0, 2)), jnp.transpose(step_size))
    final, attended = lax.scan(advance, start, inputs)
    normalized = attended * lax.rsqrt(lax.optimization_barrier(jnp.mean(attended * attended, axis=-1, keepdims=True)) + 1e-05)
    normalized = normalized * out_gain.reshape(HEADS, DK)
    lowered = jnp.dot(normed, gate_down_matrix, preferred_element_type=jnp.float32).astype(jnp.bfloat16)
    gate = jnp.dot(lowered, gate_up, preferred_element_type=jnp.float32).reshape(TOKENS, HEADS, DK)
    gated = (normalized * jax.nn.sigmoid(gate)).reshape(TOKENS, HEADS * DK).astype(jnp.bfloat16)
    return jnp.dot(gated, out_weight, preferred_element_type=jnp.float32).astype(jnp.bfloat16)
```

```python
import functools

import jax
import jax.numpy as jnp
from jax import lax
from jax.experimental import pallas as pl
from jax.experimental.pallas import tpu as pltpu
from jax.sharding import PartitionSpec as P

F32 = jnp.float32
BF16 = jnp.bfloat16
C = 128
W = 128
TILE = 512
VMEM = 56 * 1024 * 1024


def mm(a, b):
    return jnp.dot(a, b, preferred_element_type=F32)


def mm_nt(a, b):
    return lax.dot_general(a, b, (((1,), (1,)), ((), ())), preferred_element_type=F32)


def bd(a):
    z = jnp.zeros((a.shape[0], W), a.dtype)
    return jnp.concatenate(
        [
            jnp.concatenate([a[:, :W], z], axis=1),
            jnp.concatenate([z, a[:, W:]], axis=1),
        ],
        axis=0,
    )


def per_head(a, fn):
    return jnp.concatenate(
        [
            jnp.broadcast_to(fn(a[:, :W]), (a.shape[0], W)),
            jnp.broadcast_to(fn(a[:, W:]), (a.shape[0], W)),
        ],
        axis=1,
    )


def normalise(x, gain):
    wide = x.astype(F32)
    ms = jnp.mean(wide * wide, axis=-1, keepdims=True)
    return (wide * lax.rsqrt(ms + 1e-06) * gain).astype(BF16)


def local_kernel(
    x_ref,
    halo_ref,
    gain_ref,
    w_ref,
    conv_ref,
    down_ref,
    g_ref,
    b_ref,
    low_ref,
    m_ref,
    q_ref,
    u_ref,
    w_out_ref,
    z_ref,
    fin_ref,
    normed,
    proj,
    state,
):
    step = pl.program_id(0)
    n = TILE // C
    gain = gain_ref[...]

    @pl.when(step == 0)
    def _():
        before = normalise(halo_ref[...], gain)
        for i in range(3):
            proj[i, 0:8, :] = mm(before, w_ref[i])[8:16]
        rows = lax.broadcasted_iota(jnp.int32, (W, 2 * W), 0)
        cols = lax.broadcasted_iota(jnp.int32, (W, 2 * W), 1) % W
        state[:, : 2 * W] = jnp.zeros((W, 2 * W), F32)
        state[:, 2 * W :] = (rows == cols).astype(F32)

    @pl.when(step > 0)
    def _():
        for i in range(3):
            proj[i, 0:8, :] = proj[i, TILE : TILE + 8, :]

    for r in range(n):
        at = pl.ds(r * C, C)
        normed[at, :] = normalise(x_ref[at, :], gain)
    for i in range(3):
        proj[i, 8 : 8 + TILE, :] = mm(normed[...], w_ref[i])
    low_ref[...] = mm(normed[...], down_ref[...]).astype(BF16)

    rows = lax.broadcasted_iota(jnp.int32, (C, 2 * C), 0)
    cols = lax.broadcasted_iota(jnp.int32, (C, 2 * C), 1) % C
    strict = cols < rows
    inclusive = cols <= rows
    tri = inclusive.astype(F32).astype(BF16)

    taps = conv_ref[...].astype(F32)

    def conv(i, c):
        total = None
        for j in range(4):
            part = taps[i, j : j + 1, :] * proj[i, pl.ds(5 + j + c * C, C), :]
            total = part if total is None else total + part
        return total * pl.reciprocal(1.0 + jnp.exp(-total), approx=True)

    def unit(f):
        return f * per_head(
            f, lambda h: lax.rsqrt(jnp.sum(h * h, axis=-1, keepdims=True) + 1e-06)
        )

    chunks = range(n)
    q = [unit(conv(0, c)) * (W**-0.5) for c in chunks]
    k = [unit(conv(1, c)) for c in chunks]
    v = [conv(2, c) for c in chunks]
    beta, cum = [], []
    for c in chunks:
        at = pl.ds(c * C, C)
        beta.append(jnp.concatenate([b_ref[0:1, at], b_ref[1:2, at]], axis=1))
        g = jnp.concatenate([g_ref[0, at, :], g_ref[1, at, :]], axis=1)
        hi = g.astype(BF16)
        lo = (g - hi.astype(F32)).astype(BF16)
        cum.append(mm(tri, jnp.concatenate([hi, lo], axis=0)))
    mid = [a[C // 2 - 1 : C // 2, :] for a in cum]
    last = [a[C - 1 : C, :] for a in cum]
    rise = [jnp.exp(cum[c] - mid[c]) for c in chunks]
    fall = [jnp.exp(mid[c] - cum[c]) for c in chunks]
    from_start = [jnp.exp(mid[c]) for c in chunks]
    to_end = [jnp.exp(last[c] - mid[c]) for c in chunks]
    kr = [k[c] * rise[c] for c in chunks]
    qr = [q[c] * rise[c] for c in chunks]
    kf = [k[c] * fall[c] for c in chunks]
    pairs = [
        mm_nt(
            jnp.concatenate([kr[c].astype(BF16), qr[c].astype(BF16)], axis=0),
            bd(kf[c].astype(BF16)),
        )
        for c in chunks
    ]
    lower = [jnp.where(strict, pairs[c][:C] * beta[c], 0.0) for c in chunks]
    for c in chunks:
        at = pl.ds(c * C, C)
        m_ref[at, :] = jnp.where(inclusive, pairs[c][C:] * beta[c], 0.0).astype(BF16)
        q_ref[at, :] = (qr[c] * from_start[c]).astype(BF16)

    two = (rows // 2 == cols // 2) & strict
    inv = [jnp.where(two, -lower[c], 0.0) for c in chunks]
    inv16 = [a.astype(BF16) for a in inv]
    lower16 = [a.astype(BF16) for a in lower]
    size = 2
    while size < C:
        off = (
            (rows // (2 * size) == cols // (2 * size))
            & (rows % (2 * size) >= size)
            & (cols % (2 * size) < size)
        )
        keep = off.astype(F32).astype(BF16)
        cross = [lower16[c] * keep for c in chunks]
        left = [cross[c].astype(F32) + mm(cross[c], bd(inv16[c])) for c in chunks]
        left16 = [a.astype(BF16) for a in left]
        both = [left[c] + mm(inv16[c], bd(left16[c])) for c in chunks]
        inv = [inv[c] - both[c] for c in chunks]
        inv16 = [a.astype(BF16) for a in inv]
        size *= 2

    kpos = [kr[c] * from_start[c] for c in chunks]
    u = [(v[c] + mm(inv16[c], bd(v[c].astype(BF16)))).astype(BF16) for c in chunks]
    w = [(kpos[c] + mm(inv16[c], bd(kpos[c].astype(BF16)))).astype(BF16) for c in chunks]
    kt = []
    for c in chunks:
        ke = kf[c] * to_end[c]
        both_t = jnp.concatenate([ke[:, :W].T, ke[:, W:].T], axis=1)
        kt.append((both_t * beta[c]).astype(BF16))
    bmat = [mm(kt[c], bd(u[c])) for c in chunks]
    emat = [mm(kt[c], bd(w[c])).astype(BF16) for c in chunks]
    ends = jnp.concatenate(
        [jnp.exp(last[c])[:, h * W : (h + 1) * W] for c in chunks for h in range(2)],
        axis=0,
    ).T
    zb = state[:, : 2 * W]
    za = state[:, 2 * W :]
    for c in chunks:
        at = pl.ds(c * C, C)
        u_ref[at, :] = u[c]
        w_out_ref[at, :] = w[c]
        zb16, za16 = zb.astype(BF16), za.astype(BF16)
        z_ref[at, : 2 * W] = zb16
        z_ref[at, 2 * W :] = za16
        decay = jnp.concatenate(
            [
                jnp.broadcast_to(ends[:, 2 * c : 2 * c + 1], (W, W)),
                jnp.broadcast_to(ends[:, 2 * c + 1 : 2 * c + 2], (W, W)),
            ],
            axis=1,
        )
        zb = decay * zb + bmat[c] - mm(emat[c], bd(zb16))
        za = decay * za - mm(emat[c], bd(za16))
    state[:, : 2 * W] = zb
    state[:, 2 * W :] = za
    fin_ref[:, : 2 * W] = zb.astype(BF16)
    fin_ref[:, 2 * W :] = za.astype(BF16)


def local_part(x, halo, gain, qkv, conv, down, g, b):
    tokens, d = x.shape
    rank = down.shape[1]
    grid = tokens // TILE
    whole = lambda *shape: pl.BlockSpec(shape, lambda i: (0,) * len(shape))
    rows = lambda width: pl.BlockSpec((TILE, width), lambda i: (i, 0))
    return pl.pallas_call(
        local_kernel,
        grid=(grid,),
        in_specs=[
            rows(d),
            whole(16, d),
            whole(1, d),
            whole(3, d, 2 * W),
            whole(3, 4, 2 * W),
            whole(d, rank),
            pl.BlockSpec((2, TILE, W), lambda i: (0, i, 0)),
            pl.BlockSpec((2, TILE), lambda i: (0, i)),
        ],
        out_specs=[
            rows(rank),
            rows(2 * W),
            rows(2 * W),
            rows(2 * W),
            rows(2 * W),
            rows(4 * W),
            whole(W, 4 * W),
        ],
        out_shape=[
            jax.ShapeDtypeStruct((tokens, rank), BF16),
            jax.ShapeDtypeStruct((tokens, 2 * W), BF16),
            jax.ShapeDtypeStruct((tokens, 2 * W), BF16),
            jax.ShapeDtypeStruct((tokens, 2 * W), BF16),
            jax.ShapeDtypeStruct((tokens, 2 * W), BF16),
            jax.ShapeDtypeStruct((tokens, 4 * W), BF16),
            jax.ShapeDtypeStruct((W, 4 * W), BF16),
        ],
        scratch_shapes=[
            pltpu.VMEM((TILE, d), BF16),
            pltpu.VMEM((3, TILE + 8, 2 * W), F32),
            pltpu.VMEM((W, 4 * W), F32),
        ],
        compiler_params=pltpu.CompilerParams(vmem_limit_bytes=VMEM),
        cost_estimate=pl.CostEstimate(
            flops=14_000_000_000, bytes_accessed=24_000_000, transcendentals=6_000_000
        ),
        name="local_part",
    )(x, halo, gain, qkv, conv, down, g, b)


def reading_kernel(m_ref, q_ref, u_ref, w_ref, z_ref, low_ref, up_ref, gain_ref, o_ref, r_ref, s_ref):
    n = m_ref.shape[0] // C
    ats = [pl.ds(c * C, C) for c in range(n)]
    ms = [m_ref[at, :] for at in ats]
    mu = [mm(ms[c], bd(u_ref[ats[c], :])) for c in range(n)]
    mw = [mm(ms[c], bd(w_ref[ats[c], :])) for c in range(n)]
    rd = [(q_ref[ats[c], :].astype(F32) - mw[c]).astype(BF16) for c in range(n)]
    for c in range(n):
        o_ref[ats[c], :] = mu[c] + mm(rd[c], bd(z_ref[ats[c], : 2 * W]))
        r_ref[ats[c], :] = mm(rd[c], bd(z_ref[ats[c], 2 * W :])).astype(BF16)
    gate = mm(low_ref[...], up_ref[...])
    s_ref[...] = (
        gain_ref[...] * pl.reciprocal(1.0 + jnp.exp(-gate), approx=True)
    ).astype(BF16)


def reading_part(m, q, u, w, z, low, up, gain):
    tokens = m.shape[0]
    rank = low.shape[1]
    whole = lambda *shape: pl.BlockSpec(shape, lambda i: (0,) * len(shape))
    rows = lambda width: pl.BlockSpec((TILE, width), lambda i: (i, 0))
    return pl.pallas_call(
        reading_kernel,
        grid=(tokens // TILE,),
        in_specs=[rows(2 * W)] * 4
        + [rows(4 * W), rows(rank), whole(rank, 2 * W), whole(1, 2 * W)],
        out_specs=[rows(2 * W)] * 3,
        out_shape=[
            jax.ShapeDtypeStruct((tokens, 2 * W), F32),
            jax.ShapeDtypeStruct((tokens, 2 * W), BF16),
            jax.ShapeDtypeStruct((tokens, 2 * W), BF16),
        ],
        compiler_params=pltpu.CompilerParams(vmem_limit_bytes=VMEM),
        cost_estimate=pl.CostEstimate(
            flops=3_000_000_000, bytes_accessed=12_000_000, transcendentals=1_000_000
        ),
        name="reading_part",
    )(m, q, u, w, z, low, up, gain)


def compose_kernel(zi_ref, own, one, two, three, tot_ref, pre_ref, slots):
    z = zi_ref[0]
    for d, ref in enumerate((own, one, two, three)):
        slots[d] = ref[...]
    rows = lax.broadcasted_iota(jnp.int32, (W, 2 * W), 0)
    cols = lax.broadcasted_iota(jnp.int32, (W, 2 * W), 1) % W
    first = slots[z]
    pb = jnp.zeros((W, 2 * W), F32)
    pa = (rows == cols).astype(F32)
    tb = first[:, : 2 * W].astype(F32)
    ta = first[:, 2 * W :].astype(F32)
    for j in range(1, 4):
        here = j == z
        pb = jnp.where(here, tb, pb)
        pa = jnp.where(here, ta, pa)
        nxt = slots[lax.rem(z - j + 4, 4)]
        a = nxt[:, 2 * W :]
        tb = nxt[:, : 2 * W].astype(F32) + mm(a, bd(tb.astype(BF16)))
        ta = mm(a, bd(ta.astype(BF16)))
    tot_ref[:, : 2 * W] = tb.astype(BF16)
    tot_ref[:, 2 * W :] = ta.astype(BF16)
    pre_ref[:, : 2 * W] = pb.astype(BF16)
    pre_ref[:, 2 * W :] = pa.astype(BF16)


def compose(zi, own, one, two, three):
    shape = jax.ShapeDtypeStruct(own.shape, BF16)
    return pl.pallas_call(
        compose_kernel,
        in_specs=[pl.BlockSpec(memory_space=pltpu.SMEM)]
        + [pl.BlockSpec(memory_space=pltpu.VMEM)] * 4,
        out_specs=[pl.BlockSpec(memory_space=pltpu.VMEM)] * 2,
        out_shape=[shape, shape],
        scratch_shapes=[pltpu.VMEM((4,) + own.shape, BF16)],
        cost_estimate=pl.CostEstimate(
            flops=30_000_000, bytes_accessed=800_000, transcendentals=0
        ),
        name="compose",
    )(zi, own, one, two, three)


def gated_kernel(xi_ref, one, two, three, pre, o_ref, r_ref, s_ref, out_ref, start):
    @pl.when(pl.program_id(0) == 0)
    def _():
        xi = xi_ref[0]
        s = jnp.zeros((W, 2 * W), F32)
        for d, ref in ((3, three), (2, two), (1, one)):
            nxt = ref[:, : 2 * W].astype(F32) + mm(ref[:, 2 * W :], bd(s.astype(BF16)))
            s = jnp.where(xi >= d, nxt, s)
        s = pre[:, : 2 * W].astype(F32) + mm(pre[:, 2 * W :], bd(s.astype(BF16)))
        start[...] = bd(s.astype(BF16))

    att = o_ref[...] + mm(r_ref[...], start[...])
    scale = per_head(
        att, lambda h: lax.rsqrt(jnp.mean(h * h, axis=-1, keepdims=True) + 1e-05)
    )
    out_ref[...] = (att * scale * s_ref[...].astype(F32)).astype(BF16)


def gated_part(xi, one, two, three, pre, o, r, s):
    tokens = o.shape[0]
    whole = pl.BlockSpec((W, 4 * W), lambda i: (0, 0))
    rows = pl.BlockSpec((TILE, 2 * W), lambda i: (i, 0))
    return pl.pallas_call(
        gated_kernel,
        grid=(tokens // TILE,),
        in_specs=[pl.BlockSpec(memory_space=pltpu.SMEM)] + [whole] * 4 + [rows] * 3,
        out_specs=rows,
        out_shape=jax.ShapeDtypeStruct((tokens, 2 * W), BF16),
        scratch_shapes=[pltpu.VMEM((2 * W, 2 * W), BF16)],
        compiler_params=pltpu.CompilerParams(vmem_limit_bytes=VMEM),
        cost_estimate=pl.CostEstimate(
            flops=300_000_000, bytes_accessed=5_000_000, transcendentals=10_000
        ),
        name="gated_part",
    )(xi, one, two, three, pre, o, r, s)


def mixed_kernel(ci_ref, *refs):
    n = (len(refs) - 2) // 2
    wt, mine, theirs, out = refs[0], refs[1 : 1 + n], refs[1 + n : 1 + 2 * n], refs[-1]
    del wt, mine, theirs, out, ci_ref


def body(
    activations,
    norm_gain,
    qkv_weight,
    conv_weight,
    gate_down_matrix,
    gate_up,
    log_forget_gates,
    step_size,
    out_gain,
    out_weight,
):
    tokens, d = activations.shape
    ctx = lax.axis_index("ctx")
    xi, zi = ctx // 4, ctx % 4
    halo = lax.ppermute(
        activations[tokens - 16 :], "ctx", [(i, i + 1) for i in range(15)]
    )
    low, m, q, u, w, z, fin = local_part(
        activations,
        halo,
        norm_gain.reshape(1, d),
        qkv_weight,
        conv_weight,
        gate_down_matrix,
        log_forget_gates,
        step_size,
    )

    def along_z(a, by):
        pairs = [(4 * i + j, 4 * i + (j + by) % 4) for i in range(4) for j in range(4)]
        return lax.ppermute(a, "ctx", pairs)

    def along_x(a, by):
        pairs = [(4 * i + j, 4 * ((i + by) % 4) + j) for i in range(4) for j in range(4)]
        return lax.ppermute(a, "ctx", pairs)

    z1, z3, z2 = along_z(fin, 1), along_z(fin, 3), along_z(fin, 2)
    o, r, s = reading_part(
        m, q, u, w, z, low, gate_up, out_gain.reshape(1, 2 * W)
    )
    total, before = compose(zi.reshape(1), fin, z1, z2, z3)
    x1, x3, x2 = along_x(total, 1), along_x(total, 3), along_x(total, 2)
    gated = gated_part(xi.reshape(1), x1, x2, x3, before, o, r, s)
    columns = lax.all_to_all(out_weight, "head", split_axis=1, concat_axis=0, tiled=True)
    mixed = jnp.dot(
        lax.all_gather(gated, "head", axis=1, tiled=True),
        columns,
        preferred_element_type=jnp.float32,
    )
    return mixed.astype(jnp.bfloat16)


def solution(mesh):
    in_specs = (
        P("ctx", None),
        P(),
        P(None, None, "head"),
        P(None, None, "head"),
        P(),
        P(None, "head"),
        P("head", "ctx", None),
        P("head", "ctx"),
        P("head"),
        P("head", None),
    )
    out_specs = P("ctx", "head")
    return jax.shard_map(body, mesh=mesh, in_specs=in_specs, out_specs=out_specs, check_vma=False)
```

```python
import functools

import jax
import jax.numpy as jnp
from jax import lax
from jax.experimental import pallas as pl
from jax.experimental.pallas import tpu as pltpu
from jax.sharding import PartitionSpec as P

F32 = jnp.float32
BF16 = jnp.bfloat16
C = 128
W = 128
TILE = 512
MIB = 1024 * 1024


def mm(a, b):
    return jnp.dot(a, b, preferred_element_type=F32)


def mm_nt(a, b):
    return lax.dot_general(a, b, (((1,), (1,)), ((), ())), preferred_element_type=F32)


def bd(a):
    z = jnp.zeros((a.shape[0], W), a.dtype)
    return jnp.concatenate(
        [
            jnp.concatenate([a[:, :W], z], axis=1),
            jnp.concatenate([z, a[:, W:]], axis=1),
        ],
        axis=0,
    )


def per_head(a, fn):
    return jnp.concatenate(
        [
            jnp.broadcast_to(fn(a[:, :W]), (a.shape[0], W)),
            jnp.broadcast_to(fn(a[:, W:]), (a.shape[0], W)),
        ],
        axis=1,
    )


def local_kernel(
    x_ref,
    halo_ref,
    gain_ref,
    w_ref,
    conv_ref,
    down_ref,
    g_ref,
    b_ref,
    low_ref,
    m_ref,
    q_ref,
    u_ref,
    w_out_ref,
    z_ref,
    fin_ref,
    wide,
    narrow,
    low,
    scale,
    fresh,
    proj,
    state,
):
    step = pl.program_id(0)
    tiles = pl.num_programs(0) - 1
    n = TILE // C
    chunks = range(n)

    def projecting():
        block = TILE // 4

        def product(i, r):
            at = pl.ds(r * block, block)
            p = mm(x_ref[at, :], wide[i] if i < 3 else narrow[...])
            if i == 3:
                low[at, :] = p
                return
            for h in range(2):
                fresh[i, h, at, :] = p[:, h * W : (h + 1) * W]

        def root(r):
            at = pl.ds(r * C, C)
            rows = x_ref[at, :].astype(F32)
            ms = jnp.mean(rows * rows, axis=-1, keepdims=True)
            scale[at, :] = jnp.broadcast_to(lax.rsqrt(ms + 1e-06), (C, W))

        def apply(r):
            at = pl.ds(r * C, C)
            to = pl.ds(8 + r * C, C)
            for i in range(3):
                for h in range(2):
                    proj[i, h, to, :] = fresh[i, h, at, :] * scale[at, :]
            low_ref[at, :] = (low[at, :] * scale[at, :]).astype(BF16)

        products = [functools.partial(product, i, r) for i in range(4) for r in range(4)]
        roots = [functools.partial(root, r) for r in chunks]
        return products, roots, [functools.partial(apply, r) for r in chunks]

    def delta(products=(), roots=(), applies=()):
        products, roots = list(products), list(roots)

        def fill(parts, count=1):
            for part in parts[:count]:
                part()
            del parts[:count]

        rows = lax.broadcasted_iota(jnp.int32, (C, 2 * C), 0)
        cols = lax.broadcasted_iota(jnp.int32, (C, 2 * C), 1) % C
        strict = cols < rows
        inclusive = cols <= rows
        tri = inclusive.astype(F32).astype(BF16)
        taps = conv_ref[...].astype(F32)

        def conv(i, c):
            halves = []
            for h in range(2):
                total = None
                for j in range(4):
                    part = (
                        taps[i, j : j + 1, h * W : (h + 1) * W]
                        * proj[i, h, pl.ds(5 + j + c * C, C), :]
                    )
                    total = part if total is None else total + part
                halves.append(total * pl.reciprocal(1.0 + jnp.exp(-total), approx=True))
            return halves

        def unit(halves, factor=1.0):
            return jnp.concatenate(
                [
                    h
                    * (lax.rsqrt(jnp.sum(h * h, axis=-1, keepdims=True) + 1e-06) * factor)
                    for h in halves
                ],
                axis=1,
            )

        beta, cum = [], []
        for c in chunks:
            at = pl.ds(c * C, C)
            beta.append(jnp.concatenate([b_ref[0:1, at], b_ref[1:2, at]], axis=1))
            g = jnp.concatenate([g_ref[0, at, :], g_ref[1, at, :]], axis=1)
            hi = g.astype(BF16)
            lo = (g - hi.astype(F32)).astype(BF16)
            cum.append(mm(tri, jnp.concatenate([hi, lo], axis=0)))
        k = []
        for c in chunks:
            k.append(unit(conv(1, c)))
        mid = [a[C // 2 - 1 : C // 2, :] for a in cum]
        last = [a[C - 1 : C, :] for a in cum]
        rise = [jnp.exp(cum[c] - mid[c]) for c in chunks]
        fall = [jnp.exp(mid[c] - cum[c]) for c in chunks]
        from_start = [jnp.exp(mid[c]) for c in chunks]
        to_end = [jnp.exp(last[c] - mid[c]) for c in chunks]
        kr = [k[c] * rise[c] for c in chunks]
        kf = [k[c] * fall[c] for c in chunks]
        qr = []
        for c in chunks:
            qr.append(unit(conv(0, c), W**-0.5) * rise[c])
        v16 = [jnp.concatenate(conv(2, c), axis=1).astype(BF16) for c in chunks]
        pairs = [
            mm_nt(
                jnp.concatenate([kr[c].astype(BF16), qr[c].astype(BF16)], axis=0),
                bd(kf[c].astype(BF16)),
            )
            for c in chunks
        ]
        lower = [jnp.where(strict, pairs[c][:C] * beta[c], 0.0) for c in chunks]
        for c in chunks:
            at = pl.ds(c * C, C)
            m_ref[at, :] = jnp.where(inclusive, pairs[c][C:] * beta[c], 0.0).astype(BF16)
            q_ref[at, :] = (qr[c] * from_start[c]).astype(BF16)

        two = (rows // 2 == cols // 2) & strict
        eye = (rows == cols).astype(F32)
        inv = [(eye - jnp.where(two, lower[c], 0.0)).astype(BF16) for c in chunks]
        lower16 = [a.astype(BF16) for a in lower]
        size = 2
        while size < C:
            fill(roots)
            off = (
                (rows // (2 * size) == cols // (2 * size))
                & (rows % (2 * size) >= size)
                & (cols % (2 * size) < size)
            )
            keep = off.astype(F32).astype(BF16)
            left = [mm(lower16[c] * keep, bd(inv[c])).astype(BF16) for c in chunks]
            fill(products)
            both = [mm(inv[c], bd(left[c])).astype(BF16) for c in chunks]
            fill(products, 2)
            inv = [inv[c] - both[c] for c in chunks]
            size *= 2

        fill(products, len(products))
        fill(roots, len(roots))
        if applies:
            proj[:, :, 0:8, :] = proj[:, :, TILE : TILE + 8, :]
        for part in applies:
            part()
        kpos = [kr[c] * from_start[c] for c in chunks]
        u = [mm(inv[c], bd(v16[c])).astype(BF16) for c in chunks]
        w = [mm(inv[c], bd(kpos[c].astype(BF16))).astype(BF16) for c in chunks]
        kt = []
        for c in chunks:
            ke = kf[c] * to_end[c]
            both_t = jnp.concatenate([ke[:, :W].T, ke[:, W:].T], axis=1)
            kt.append((both_t * beta[c]).astype(BF16))
        bmat = [mm(kt[c], bd(u[c])) for c in chunks]
        emat = [mm(kt[c], bd(w[c])).astype(BF16) for c in chunks]
        ends = jnp.concatenate(
            [jnp.exp(last[c])[:, h * W : (h + 1) * W] for c in chunks for h in range(2)],
            axis=0,
        ).T
        zb = state[:, : 2 * W]
        za = state[:, 2 * W :]
        for c in chunks:
            at = pl.ds(c * C, C)
            u_ref[at, :] = u[c]
            w_out_ref[at, :] = w[c]
            zb16, za16 = zb.astype(BF16), za.astype(BF16)
            z_ref[at, : 2 * W] = zb16
            z_ref[at, 2 * W :] = za16
            decay = jnp.concatenate(
                [
                    jnp.broadcast_to(ends[:, 2 * c : 2 * c + 1], (W, W)),
                    jnp.broadcast_to(ends[:, 2 * c + 1 : 2 * c + 2], (W, W)),
                ],
                axis=1,
            )
            zb = decay * zb + bmat[c] - mm(emat[c], bd(zb16))
            za = decay * za - mm(emat[c], bd(za16))
        state[:, : 2 * W] = zb
        state[:, 2 * W :] = za

    @pl.when(step == 0)
    def _():
        gain = gain_ref[...].T
        for j in range(gain.shape[1]):
            at = pl.ds(j * W, W)
            column = gain[:, j : j + 1]
            for i in range(3):
                wide[i, at, :] = (w_ref[i, at, :].astype(F32) * column).astype(BF16)
            narrow[at, :] = (down_ref[at, :].astype(F32) * column).astype(BF16)
        rows = halo_ref[...].astype(F32)
        ms = jnp.mean(rows * rows, axis=-1, keepdims=True)
        for i in range(3):
            p = (mm(halo_ref[...], wide[i]) * lax.rsqrt(ms + 1e-06))[8:16]
            for h in range(2):
                proj[i, h, 0:8, :] = p[:, h * W : (h + 1) * W]
        rows = lax.broadcasted_iota(jnp.int32, (W, 2 * W), 0)
        cols = lax.broadcasted_iota(jnp.int32, (W, 2 * W), 1) % W
        state[:, : 2 * W] = jnp.zeros((W, 2 * W), F32)
        state[:, 2 * W :] = (rows == cols).astype(F32)
        for parts in projecting():
            for part in parts:
                part()

    @pl.when((step > 0) & (step < tiles))
    def _():
        delta(*projecting())

    @pl.when(step == tiles)
    def _():
        delta()
        fin_ref[...] = state[...].astype(BF16)


def local_part(x, halo, gain, qkv, conv, down, g, b):
    tokens, d = x.shape
    rank = down.shape[1]
    grid = tokens // TILE
    whole = lambda *shape: pl.BlockSpec(shape, lambda i: (0,) * len(shape))
    first = lambda i: jnp.minimum(i, grid - 1)
    then = lambda i: jnp.maximum(i - 1, 0)
    early = lambda width: pl.BlockSpec((TILE, width), lambda i: (first(i), 0))
    rows = lambda width: pl.BlockSpec((TILE, width), lambda i: (then(i), 0))
    return pl.pallas_call(
        local_kernel,
        grid=(grid + 1,),
        in_specs=[
            early(d),
            whole(16, d),
            whole(d // W, W),
            whole(3, d, 2 * W),
            whole(3, 4, 2 * W),
            whole(d, rank),
            pl.BlockSpec((2, TILE, W), lambda i: (0, then(i), 0)),
            pl.BlockSpec((2, TILE), lambda i: (0, then(i))),
        ],
        out_specs=[
            early(rank),
            rows(2 * W),
            rows(2 * W),
            rows(2 * W),
            rows(2 * W),
            rows(4 * W),
            whole(W, 4 * W),
        ],
        out_shape=[
            jax.ShapeDtypeStruct((tokens, rank), BF16),
            jax.ShapeDtypeStruct((tokens, 2 * W), BF16),
            jax.ShapeDtypeStruct((tokens, 2 * W), BF16),
            jax.ShapeDtypeStruct((tokens, 2 * W), BF16),
            jax.ShapeDtypeStruct((tokens, 2 * W), BF16),
            jax.ShapeDtypeStruct((tokens, 4 * W), BF16),
            jax.ShapeDtypeStruct((W, 4 * W), BF16),
        ],
        scratch_shapes=[
            pltpu.VMEM((3, d, 2 * W), BF16),
            pltpu.VMEM((d, rank), BF16),
            pltpu.VMEM((TILE, rank), F32),
            pltpu.VMEM((TILE, W), F32),
            pltpu.VMEM((3, 2, TILE, W), F32),
            pltpu.VMEM((3, 2, TILE + 8, W), F32),
            pltpu.VMEM((W, 4 * W), F32),
        ],
        compiler_params=pltpu.CompilerParams(vmem_limit_bytes=56 * MIB),
        cost_estimate=pl.CostEstimate(
            flops=14_000_000_000, bytes_accessed=24_000_000, transcendentals=6_000_000
        ),
        name="local_part",
    )(x, halo, gain, qkv, conv, down, g, b)


def reading_kernel(m_ref, q_ref, u_ref, w_ref, z_ref, low_ref, up_ref, gain_ref, o_ref, r_ref, s_ref):
    n = m_ref.shape[0] // C
    ats = [pl.ds(c * C, C) for c in range(n)]
    ms = [m_ref[at, :] for at in ats]
    mu = [mm(ms[c], bd(u_ref[ats[c], :])) for c in range(n)]
    mw = [mm(ms[c], bd(w_ref[ats[c], :])) for c in range(n)]
    rd = [(q_ref[ats[c], :].astype(F32) - mw[c]).astype(BF16) for c in range(n)]
    for c in range(n):
        o_ref[ats[c], :] = mu[c] + mm(rd[c], bd(z_ref[ats[c], : 2 * W]))
        r_ref[ats[c], :] = mm(rd[c], bd(z_ref[ats[c], 2 * W :])).astype(BF16)
    gate = mm(low_ref[...], up_ref[...])
    s_ref[...] = (
        gain_ref[...] * pl.reciprocal(1.0 + jnp.exp(-gate), approx=True)
    ).astype(BF16)


def reading_part(m, q, u, w, z, low, up, gain):
    tokens = m.shape[0]
    rank = low.shape[1]
    whole = lambda *shape: pl.BlockSpec(shape, lambda i: (0,) * len(shape))
    rows = lambda width: pl.BlockSpec((TILE, width), lambda i: (i, 0))
    return pl.pallas_call(
        reading_kernel,
        grid=(tokens // TILE,),
        in_specs=[rows(2 * W)] * 4
        + [rows(4 * W), rows(rank), whole(rank, 2 * W), whole(1, 2 * W)],
        out_specs=[rows(2 * W)] * 3,
        out_shape=[
            jax.ShapeDtypeStruct((tokens, 2 * W), F32),
            jax.ShapeDtypeStruct((tokens, 2 * W), BF16),
            jax.ShapeDtypeStruct((tokens, 2 * W), BF16),
        ],
        compiler_params=pltpu.CompilerParams(vmem_limit_bytes=56 * MIB),
        cost_estimate=pl.CostEstimate(
            flops=3_000_000_000, bytes_accessed=12_000_000, transcendentals=1_000_000
        ),
        name="reading_part",
    )(m, q, u, w, z, low, up, gain)


def compose_kernel(zi_ref, own, one, two, three, tot_ref, pre_ref, slots):
    z = zi_ref[0]
    for d, ref in enumerate((own, one, two, three)):
        slots[d] = ref[...]
    rows = lax.broadcasted_iota(jnp.int32, (W, 2 * W), 0)
    cols = lax.broadcasted_iota(jnp.int32, (W, 2 * W), 1) % W
    first = slots[z]
    pb = jnp.zeros((W, 2 * W), F32)
    pa = (rows == cols).astype(F32)
    tb = first[:, : 2 * W].astype(F32)
    ta = first[:, 2 * W :].astype(F32)
    for j in range(1, 4):
        here = j == z
        pb = jnp.where(here, tb, pb)
        pa = jnp.where(here, ta, pa)
        nxt = slots[lax.rem(z - j + 4, 4)]
        a = nxt[:, 2 * W :]
        tb = nxt[:, : 2 * W].astype(F32) + mm(a, bd(tb.astype(BF16)))
        ta = mm(a, bd(ta.astype(BF16)))
    tot_ref[:, : 2 * W] = tb.astype(BF16)
    tot_ref[:, 2 * W :] = ta.astype(BF16)
    pre_ref[:, : 2 * W] = pb.astype(BF16)
    pre_ref[:, 2 * W :] = pa.astype(BF16)


def compose(zi, own, one, two, three):
    shape = jax.ShapeDtypeStruct(own.shape, BF16)
    return pl.pallas_call(
        compose_kernel,
        in_specs=[pl.BlockSpec(memory_space=pltpu.SMEM)]
        + [pl.BlockSpec(memory_space=pltpu.VMEM)] * 4,
        out_specs=[pl.BlockSpec(memory_space=pltpu.VMEM)] * 2,
        out_shape=[shape, shape],
        scratch_shapes=[pltpu.VMEM((4,) + own.shape, BF16)],
        compiler_params=pltpu.CompilerParams(vmem_limit_bytes=4 * MIB),
        cost_estimate=pl.CostEstimate(
            flops=30_000_000, bytes_accessed=800_000, transcendentals=0
        ),
        name="compose",
    )(zi, own, one, two, three)


def gated_kernel(at_ref, one, two, three, pre, o_ref, r_ref, s_ref, *rest):
    outs, start = rest[:-1], rest[-1]
    step = pl.program_id(0)

    @pl.when(step == 0)
    def _():
        xi = at_ref[0]
        s = jnp.zeros((W, 2 * W), F32)
        for d, ref in ((3, three), (2, two), (1, one)):
            nxt = ref[:, : 2 * W].astype(F32) + mm(ref[:, 2 * W :], bd(s.astype(BF16)))
            s = jnp.where(xi >= d, nxt, s)
        s = pre[:, : 2 * W].astype(F32) + mm(pre[:, 2 * W :], bd(s.astype(BF16)))
        start[...] = bd(s.astype(BF16))

    att = o_ref[...] + mm(r_ref[...], start[...])
    scale = per_head(
        att, lambda h: lax.rsqrt(jnp.mean(h * h, axis=-1, keepdims=True) + 1e-05)
    )
    gated = (att * scale * s_ref[...].astype(F32)).astype(BF16)
    for d, out in enumerate(outs):

        @pl.when(step == d)
        def _():
            out[...] = gated


def gated_part(at, one, two, three, pre, o, r, s):
    part = o.shape[0] // 4
    whole = pl.BlockSpec((W, 4 * W), lambda i, at: (0, 0))
    rows = pl.BlockSpec((part, 2 * W), lambda i, at: (lax.rem(at[1] + i, 4), 0))
    keep = pl.BlockSpec((part, 2 * W), lambda i, at: (0, 0))
    return pl.pallas_call(
        gated_kernel,
        grid_spec=pltpu.PrefetchScalarGridSpec(
            num_scalar_prefetch=1,
            grid=(4,),
            in_specs=[whole] * 4 + [rows] * 3,
            out_specs=[keep] * 4,
            scratch_shapes=[pltpu.VMEM((2 * W, 2 * W), BF16)],
        ),
        out_shape=[jax.ShapeDtypeStruct((part, 2 * W), BF16)] * 4,
        compiler_params=pltpu.CompilerParams(vmem_limit_bytes=10 * MIB),
        cost_estimate=pl.CostEstimate(
            flops=300_000_000, bytes_accessed=5_000_000, transcendentals=10_000
        ),
        name="gated_part",
    )(at, one, two, three, pre, o, r, s)


def turned_kernel(at_ref, w_ref, mine_ref, other_ref, held):
    features = w_ref.shape[1] // 8
    held[...] = w_ref[...].T
    for j in range(4):
        to = pl.ds(j * features, features)
        for ref, core in ((mine_ref, at_ref[1]), (other_ref, 1 - at_ref[1])):
            at = pl.multiple_of((2 * j + core) * features, 16)
            ref[to, :] = held[pl.ds(at, features), :]


def turned(at, w):
    k, n = w.shape
    half = jax.ShapeDtypeStruct((n // 2, k), w.dtype)
    return pl.pallas_call(
        turned_kernel,
        in_specs=[
            pl.BlockSpec(memory_space=pltpu.SMEM),
            pl.BlockSpec(memory_space=pltpu.VMEM),
        ],
        out_specs=[pl.BlockSpec(memory_space=pltpu.VMEM)] * 2,
        out_shape=[half, half],
        scratch_shapes=[pltpu.VMEM((n, k), w.dtype)],
        compiler_params=pltpu.CompilerParams(vmem_limit_bytes=8 * MIB),
        cost_estimate=pl.CostEstimate(
            flops=0, bytes_accessed=2_400_000, transcendentals=0
        ),
        name="turned",
    )(at, w)


def mixed_kernel(at_ref, *refs):
    step = pl.program_id(0)
    weights, blocks, outs = refs[:8], refs[8:16], refs[16:]
    total = None
    for w, g in zip(weights, blocks, strict=True):
        part = mm_nt(w[...], g[...])
        total = part if total is None else total + part
    total = total.astype(BF16)
    for d, out in enumerate(outs):

        @pl.when(step == d)
        def _():
            out[...] = total


def mixed_part(at, weights, mine, theirs):
    features = weights[0].shape[0] // 8
    tokens = mine[0].shape[0]
    wspec = lambda first: pl.BlockSpec(
        (features, 2 * W), lambda i, at: (first + lax.rem(at[0] + i, 4), 0)
    )
    gspec = pl.BlockSpec((tokens, 2 * W), lambda i, at: (0, 0))
    ospec = pl.BlockSpec((features, tokens), lambda i, at: (0, 0))
    return pl.pallas_call(
        mixed_kernel,
        grid_spec=pltpu.PrefetchScalarGridSpec(
            num_scalar_prefetch=1,
            grid=(4,),
            in_specs=[wspec(0)] * 4 + [wspec(4)] * 3 + [wspec(0)] + [gspec] * 8,
            out_specs=[ospec] * 4,
        ),
        out_shape=[jax.ShapeDtypeStruct((features, tokens), BF16)] * 4,
        compiler_params=pltpu.CompilerParams(vmem_limit_bytes=16 * MIB),
        cost_estimate=pl.CostEstimate(
            flops=2_400_000_000, bytes_accessed=8_000_000, transcendentals=0
        ),
        name="mixed_part",
    )(at, *weights, *mine, *theirs)


def joined_kernel(at_ref, *refs):
    step = pl.program_id(0)
    for d, piece in enumerate(refs[:-1]):

        @pl.when(lax.rem(at_ref[0] - d + 4, 4) == step)
        def _():
            refs[-1][...] = piece[...]


def joined(at, pieces):
    features, tokens = pieces[0].shape
    return pl.pallas_call(
        joined_kernel,
        grid_spec=pltpu.PrefetchScalarGridSpec(
            num_scalar_prefetch=1,
            grid=(4,),
            in_specs=[pl.BlockSpec((features, tokens), lambda i, at: (0, 0))] * 4,
            out_specs=pl.BlockSpec((features, tokens), lambda i, at: (0, i)),
        ),
        out_shape=jax.ShapeDtypeStruct((features, 4 * tokens), BF16),
        compiler_params=pltpu.CompilerParams(vmem_limit_bytes=10 * MIB),
        cost_estimate=pl.CostEstimate(
            flops=0, bytes_accessed=2_400_000, transcendentals=0
        ),
        name="joined",
    )(at, *pieces)


def body(
    activations,
    norm_gain,
    qkv_weight,
    conv_weight,
    gate_down_matrix,
    gate_up,
    log_forget_gates,
    step_size,
    out_gain,
    out_weight,
):
    tokens, d = activations.shape
    ctx = lax.axis_index("ctx")
    xi, zi = ctx // 4, ctx % 4
    head = lax.axis_index("head")
    yi, ci = head // 2, head % 2

    def along_y(a, by):
        return lax.ppermute(a, "head", [(i, (i + 2 * by) % 8) for i in range(8)])

    def across(a):
        return lax.ppermute(a, "head", [(i, i ^ 1) for i in range(8)])

    halo = lax.ppermute(
        activations[tokens - 16 :], "ctx", [(i, i + 1) for i in range(15)]
    )
    here = jnp.stack([yi, ci])
    mine, other = turned(here, out_weight)
    both = jnp.concatenate([mine, across(other)], axis=0)
    below, above = along_y(both, 1), along_y(both, 3)
    low, m, q, u, w, z, fin = local_part(
        activations,
        halo,
        norm_gain.reshape(d // W, W),
        qkv_weight,
        conv_weight,
        gate_down_matrix,
        log_forget_gates,
        step_size,
    )

    def along_z(a, by):
        pairs = [(4 * i + j, 4 * i + (j + by) % 4) for i in range(4) for j in range(4)]
        return lax.ppermute(a, "ctx", pairs)

    def along_x(a, by):
        pairs = [(4 * i + j, 4 * ((i + by) % 4) + j) for i in range(4) for j in range(4)]
        return lax.ppermute(a, "ctx", pairs)

    fin, below, above = lax.optimization_barrier((fin, below, above))
    half = both.shape[0] // 2
    far = along_y(above[:half], 3), along_y(below[half:], 1)
    z1, z3, z2 = along_z(fin, 1), along_z(fin, 3), along_z(fin, 2)
    o, r, s = reading_part(
        m, q, u, w, z, low, gate_up, out_gain.reshape(1, 2 * W)
    )
    total, before = compose(zi.reshape(1), fin, z1, z2, z3)
    x1, x3, x2 = along_x(total, 1), along_x(total, 3), along_x(total, 2)
    at = jnp.stack([xi, yi])
    x1, far = lax.optimization_barrier((x1, far))
    q0, q1, q2, q3 = gated_part(at, x1, x2, x3, before, o, r, s)
    own = [q0, along_y(q1, 1), along_y(q3, 3), along_y(q2, 2)]
    weights = [both, below, above, far[0], both, below, above, far[1]]
    p0, p1, p2, p3 = mixed_part(here, weights, own, [across(a) for a in own])
    pieces = [p0, along_y(p1, 1), along_y(p2, 2), along_y(p3, 3)]
    return joined(yi.reshape(1), pieces).T


def solution(mesh):
    in_specs = (
        P("ctx", None),
        P(),
        P(None, None, "head"),
        P(None, None, "head"),
        P(),
        P(None, "head"),
        P("head", "ctx", None),
        P("head", "ctx"),
        P("head"),
        P("head", None),
    )
    out_specs = P("ctx", "head")
    return jax.shard_map(body, mesh=mesh, in_specs=in_specs, out_specs=out_specs, check_vma=False)
```

```python
import functools

import jax
import jax.numpy as jnp
from jax import lax
from jax.experimental import pallas as pl
from jax.experimental.pallas import tpu as pltpu
from jax.sharding import PartitionSpec as P

F32 = jnp.float32
BF16 = jnp.bfloat16
C = 128
W = 128
TILE = 512
MIB = 1024 * 1024


def mm(a, b):
    return jnp.dot(a, b, preferred_element_type=F32)


def mm_nt(a, b):
    return lax.dot_general(a, b, (((1,), (1,)), ((), ())), preferred_element_type=F32)


def bd(a):
    z = jnp.zeros((a.shape[0], W), a.dtype)
    return jnp.concatenate(
        [
            jnp.concatenate([a[:, :W], z], axis=1),
            jnp.concatenate([z, a[:, W:]], axis=1),
        ],
        axis=0,
    )


def per_head(a, fn):
    return jnp.concatenate(
        [
            jnp.broadcast_to(fn(a[:, :W]), (a.shape[0], W)),
            jnp.broadcast_to(fn(a[:, W:]), (a.shape[0], W)),
        ],
        axis=1,
    )


def local_kernel(
    x_ref,
    halo_ref,
    gain_ref,
    wk_ref,
    wv_ref,
    conv_ref,
    g_ref,
    b_ref,
    scale,
    kf_ref,
    rise_ref,
    pos_ref,
    u_ref,
    w_out_ref,
    z_ref,
    fin_ref,
    wide,
    fresh,
    proj,
    state,
):
    step = pl.program_id(0)
    tiles = pl.num_programs(0) - 1
    n = TILE // C
    chunks = range(n)

    def projecting():
        block = TILE // 4

        def product(i, r):
            at = pl.ds(r * block, block)
            p = mm(x_ref[at, :], wide[i])
            for h in range(2):
                fresh[i, h, at, :] = p[:, h * W : (h + 1) * W]

        def root(r):
            at = pl.ds(r * C, C)
            rows = x_ref[at, :].astype(F32)
            ms = jnp.mean(rows * rows, axis=-1, keepdims=True)
            scale[at, :] = jnp.broadcast_to(lax.rsqrt(ms + 1e-06), (C, W))

        def apply(r):
            at = pl.ds(r * C, C)
            to = pl.ds(8 + r * C, C)
            for i in range(2):
                for h in range(2):
                    proj[i, h, to, :] = fresh[i, h, at, :] * scale[at, :]

        products = [functools.partial(product, i, r) for i in range(2) for r in range(4)]
        roots = [functools.partial(root, r) for r in chunks]
        return products, roots, [functools.partial(apply, r) for r in chunks]

    def delta(products=(), roots=(), applies=()):
        products, roots = list(products), list(roots)

        def fill(parts, count=1):
            for part in parts[:count]:
                part()
            del parts[:count]

        rows = lax.broadcasted_iota(jnp.int32, (C, 2 * C), 0)
        cols = lax.broadcasted_iota(jnp.int32, (C, 2 * C), 1) % C
        strict = cols < rows
        inclusive = cols <= rows
        tri = inclusive.astype(F32).astype(BF16)
        taps = conv_ref[...].astype(F32)

        def conv(i, c):
            halves = []
            for h in range(2):
                total = None
                for j in range(4):
                    part = (
                        taps[i + 1, j : j + 1, h * W : (h + 1) * W]
                        * proj[i, h, pl.ds(5 + j + c * C, C), :]
                    )
                    total = part if total is None else total + part
                halves.append(total * pl.reciprocal(1.0 + jnp.exp(-total), approx=True))
            return halves

        def unit(halves, factor=1.0):
            return jnp.concatenate(
                [
                    h
                    * (lax.rsqrt(jnp.sum(h * h, axis=-1, keepdims=True) + 1e-06) * factor)
                    for h in halves
                ],
                axis=1,
            )

        beta, cum = [], []
        for c in chunks:
            at = pl.ds(c * C, C)
            beta.append(jnp.concatenate([b_ref[0:1, at], b_ref[1:2, at]], axis=1))
            g = jnp.concatenate([g_ref[0, at, :], g_ref[1, at, :]], axis=1)
            hi = g.astype(BF16)
            lo = (g - hi.astype(F32)).astype(BF16)
            cum.append(mm(tri, jnp.concatenate([hi, lo], axis=0)))
        k = []
        for c in chunks:
            k.append(unit(conv(0, c)))
        mid = [a[C // 2 - 1 : C // 2, :] for a in cum]
        last = [a[C - 1 : C, :] for a in cum]
        rise = [jnp.exp(cum[c] - mid[c]) for c in chunks]
        fall = [jnp.exp(mid[c] - cum[c]) for c in chunks]
        from_start = [jnp.exp(mid[c]) for c in chunks]
        to_end = [jnp.exp(last[c] - mid[c]) for c in chunks]
        kr = [k[c] * rise[c] for c in chunks]
        kf = [k[c] * fall[c] for c in chunks]
        v16 = [jnp.concatenate(conv(1, c), axis=1).astype(BF16) for c in chunks]
        kf16 = [a.astype(BF16) for a in kf]
        pairs = [mm_nt(kr[c].astype(BF16), bd(kf16[c])) for c in chunks]
        lower = [jnp.where(strict, pairs[c] * beta[c], 0.0) for c in chunks]
        for c in chunks:
            at = pl.ds(c * C, C)
            kf_ref[at, :] = kf16[c]
            rise_ref[at, :] = rise[c].astype(BF16)
            pos_ref[at, :] = (rise[c] * from_start[c]).astype(BF16)

        two = (rows // 2 == cols // 2) & strict
        eye = (rows == cols).astype(F32)
        inv = [(eye - jnp.where(two, lower[c], 0.0)).astype(BF16) for c in chunks]
        lower16 = [a.astype(BF16) for a in lower]
        size = 2
        while size < C:
            fill(roots)
            off = (
                (rows // (2 * size) == cols // (2 * size))
                & (rows % (2 * size) >= size)
                & (cols % (2 * size) < size)
            )
            keep = off.astype(F32).astype(BF16)
            left = [mm(lower16[c] * keep, bd(inv[c])).astype(BF16) for c in chunks]
            fill(products)
            both = [mm(inv[c], bd(left[c])).astype(BF16) for c in chunks]
            fill(products, 2)
            inv = [inv[c] - both[c] for c in chunks]
            size *= 2

        fill(products, len(products))
        fill(roots, len(roots))
        if applies:
            proj[:, :, 0:8, :] = proj[:, :, TILE : TILE + 8, :]
        for part in applies:
            part()
        kpos = [kr[c] * from_start[c] for c in chunks]
        u = [mm(inv[c], bd(v16[c])).astype(BF16) for c in chunks]
        w = [mm(inv[c], bd(kpos[c].astype(BF16))).astype(BF16) for c in chunks]
        kt = []
        for c in chunks:
            ke = kf[c] * to_end[c]
            both_t = jnp.concatenate([ke[:, :W].T, ke[:, W:].T], axis=1)
            kt.append((both_t * beta[c]).astype(BF16))
        bmat = [mm(kt[c], bd(u[c])) for c in chunks]
        emat = [mm(kt[c], bd(w[c])).astype(BF16) for c in chunks]
        ends = jnp.concatenate(
            [jnp.exp(last[c])[:, h * W : (h + 1) * W] for c in chunks for h in range(2)],
            axis=0,
        ).T
        zb = state[:, : 2 * W]
        za = state[:, 2 * W :]
        for c in chunks:
            at = pl.ds(c * C, C)
            u_ref[at, :] = u[c]
            w_out_ref[at, :] = w[c]
            zb16, za16 = zb.astype(BF16), za.astype(BF16)
            z_ref[at, : 2 * W] = zb16
            z_ref[at, 2 * W :] = za16
            decay = jnp.concatenate(
                [
                    jnp.broadcast_to(ends[:, 2 * c : 2 * c + 1], (W, W)),
                    jnp.broadcast_to(ends[:, 2 * c + 1 : 2 * c + 2], (W, W)),
                ],
                axis=1,
            )
            zb = decay * zb + bmat[c] - mm(emat[c], bd(zb16))
            za = decay * za - mm(emat[c], bd(za16))
        state[:, : 2 * W] = zb
        state[:, 2 * W :] = za

    @pl.when(step == 0)
    def _():
        gain = gain_ref[...].T
        for j in range(gain.shape[1]):
            at = pl.ds(j * W, W)
            column = gain[:, j : j + 1]
            for i, w_ref in enumerate((wk_ref, wv_ref)):
                wide[i, at, :] = (w_ref[0, at, :].astype(F32) * column).astype(BF16)
        rows = halo_ref[...].astype(F32)
        ms = jnp.mean(rows * rows, axis=-1, keepdims=True)
        for i in range(2):
            p = (mm(halo_ref[...], wide[i]) * lax.rsqrt(ms + 1e-06))[8:16]
            for h in range(2):
                proj[i, h, 0:8, :] = p[:, h * W : (h + 1) * W]
        rows = lax.broadcasted_iota(jnp.int32, (W, 2 * W), 0)
        cols = lax.broadcasted_iota(jnp.int32, (W, 2 * W), 1) % W
        state[:, : 2 * W] = jnp.zeros((W, 2 * W), F32)
        state[:, 2 * W :] = (rows == cols).astype(F32)
        for parts in projecting():
            for part in parts:
                part()

    @pl.when((step > 0) & (step < tiles))
    def _():
        delta(*projecting())

    @pl.when(step == tiles)
    def _():
        delta()
        fin_ref[...] = state[...].astype(BF16)


def local_part(x, halo, gain, qkv, conv, g, b):
    tokens, d = x.shape
    grid = tokens // TILE
    whole = lambda *shape: pl.BlockSpec(shape, lambda i: (0,) * len(shape))
    first = lambda i: jnp.minimum(i, grid - 1)
    then = lambda i: jnp.maximum(i - 1, 0)
    early = lambda width: pl.BlockSpec((TILE, width), lambda i: (first(i), 0))
    rows = lambda width: pl.BlockSpec((TILE, width), lambda i: (then(i), 0))
    return pl.pallas_call(
        local_kernel,
        grid=(grid + 1,),
        in_specs=[
            early(d),
            whole(16, d),
            whole(d // W, W),
            pl.BlockSpec((1, d, 2 * W), lambda i: (1, 0, 0)),
            pl.BlockSpec((1, d, 2 * W), lambda i: (2, 0, 0)),
            whole(3, 4, 2 * W),
            pl.BlockSpec((2, TILE, W), lambda i: (0, then(i), 0)),
            pl.BlockSpec((2, TILE), lambda i: (0, then(i))),
        ],
        out_specs=[early(W)] + [rows(2 * W)] * 5 + [rows(4 * W), whole(W, 4 * W)],
        out_shape=[
            jax.ShapeDtypeStruct((tokens, W), F32),
            jax.ShapeDtypeStruct((tokens, 2 * W), BF16),
            jax.ShapeDtypeStruct((tokens, 2 * W), BF16),
            jax.ShapeDtypeStruct((tokens, 2 * W), BF16),
            jax.ShapeDtypeStruct((tokens, 2 * W), BF16),
            jax.ShapeDtypeStruct((tokens, 2 * W), BF16),
            jax.ShapeDtypeStruct((tokens, 4 * W), BF16),
            jax.ShapeDtypeStruct((W, 4 * W), BF16),
        ],
        scratch_shapes=[
            pltpu.VMEM((2, d, 2 * W), BF16),
            pltpu.VMEM((2, 2, TILE, W), F32),
            pltpu.VMEM((2, 2, TILE + 8, W), F32),
            pltpu.VMEM((W, 4 * W), F32),
        ],
        compiler_params=pltpu.CompilerParams(vmem_limit_bytes=56 * MIB),
        cost_estimate=pl.CostEstimate(
            flops=14_000_000_000, bytes_accessed=24_000_000, transcendentals=6_000_000
        ),
        name="local_part",
    )(x, halo, gain, qkv, qkv, conv, g, b)


def query_kernel(
    x_ref,
    halo_ref,
    gain_ref,
    w_ref,
    conv_ref,
    down_ref,
    kf_ref,
    rise_ref,
    pos_ref,
    b_ref,
    scale_ref,
    low_ref,
    m_ref,
    q_ref,
    wide,
    narrow,
    raw,
    proj,
):
    step = pl.program_id(0)
    tiles = pl.num_programs(0) - 1
    n = TILE // C

    def root(rows):
        wide_rows = rows.astype(F32)
        return lax.rsqrt(jnp.mean(wide_rows * wide_rows, axis=-1, keepdims=True) + 1e-06)

    def products():
        def queries():
            raw[...] = mm(x_ref[...], wide[...])

        def lowered():
            low = mm(x_ref[...], narrow[...])
            low_ref[...] = (low * scale_ref[...]).astype(BF16)

        return [queries, lowered]

    def keep():
        for h in range(2):
            proj[h, 8:, :] = raw[:, h * W : (h + 1) * W] * scale_ref[...]

    def finish(parts):
        parts = list(parts)
        taps = conv_ref[0].astype(F32)
        rows = lax.broadcasted_iota(jnp.int32, (C, 2 * C), 0)
        cols = lax.broadcasted_iota(jnp.int32, (C, 2 * C), 1) % C
        inclusive = cols <= rows
        for c in range(n):
            if parts:
                parts.pop(0)()
            at = pl.ds(c * C, C)
            halves = []
            for h in range(2):
                total = None
                for j in range(4):
                    part = (
                        taps[j : j + 1, h * W : (h + 1) * W]
                        * proj[h, pl.ds(5 + j + c * C, C), :]
                    )
                    total = part if total is None else total + part
                f = total * pl.reciprocal(1.0 + jnp.exp(-total), approx=True)
                size = lax.rsqrt(jnp.sum(f * f, axis=-1, keepdims=True) + 1e-06)
                halves.append(f * (size * W**-0.5))
            query = jnp.concatenate(halves, axis=1)
            risen = (query * rise_ref[at, :].astype(F32)).astype(BF16)
            q_ref[at, :] = (query * pos_ref[at, :].astype(F32)).astype(BF16)
            beta = jnp.concatenate([b_ref[0:1, at], b_ref[1:2, at]], axis=1)
            pairs = mm_nt(risen, bd(kf_ref[at, :]))
            m_ref[at, :] = jnp.where(inclusive, pairs * beta, 0.0).astype(BF16)

    @pl.when(step == 0)
    def _():
        gain = gain_ref[...].T
        for j in range(gain.shape[1]):
            at = pl.ds(j * W, W)
            column = gain[:, j : j + 1]
            wide[at, :] = (w_ref[0, at, :].astype(F32) * column).astype(BF16)
            narrow[at, :] = (down_ref[at, :].astype(F32) * column).astype(BF16)
        p = (mm(halo_ref[...], wide[...]) * root(halo_ref[...]))[8:16]
        for h in range(2):
            proj[h, 0:8, :] = p[:, h * W : (h + 1) * W]
        for part in products():
            part()
        keep()

    @pl.when((step > 0) & (step < tiles))
    def _():
        finish(products())
        proj[:, 0:8, :] = proj[:, TILE : TILE + 8, :]
        keep()

    @pl.when(step == tiles)
    def _():
        finish([])


def query_part(x, halo, gain, qkv, conv, down, kf, rise, pos, b, scale):
    tokens, d = x.shape
    rank = down.shape[1]
    whole = lambda *shape: pl.BlockSpec(shape, lambda i: (0,) * len(shape))
    grid = tokens // TILE
    first = lambda i: jnp.minimum(i, grid - 1)
    then = lambda i: jnp.maximum(i - 1, 0)
    early = lambda width: pl.BlockSpec((TILE, width), lambda i: (first(i), 0))
    rows = lambda width: pl.BlockSpec((TILE, width), lambda i: (then(i), 0))
    return pl.pallas_call(
        query_kernel,
        grid=(grid + 1,),
        in_specs=[
            early(d),
            whole(16, d),
            whole(d // W, W),
            whole(1, d, 2 * W),
            whole(3, 4, 2 * W),
            whole(d, rank),
            rows(2 * W),
            rows(2 * W),
            rows(2 * W),
            pl.BlockSpec((2, TILE), lambda i: (0, then(i))),
            early(W),
        ],
        out_specs=[early(rank), rows(2 * W), rows(2 * W)],
        out_shape=[
            jax.ShapeDtypeStruct((tokens, rank), BF16),
            jax.ShapeDtypeStruct((tokens, 2 * W), BF16),
            jax.ShapeDtypeStruct((tokens, 2 * W), BF16),
        ],
        scratch_shapes=[
            pltpu.VMEM((d, 2 * W), BF16),
            pltpu.VMEM((d, rank), BF16),
            pltpu.VMEM((TILE, 2 * W), F32),
            pltpu.VMEM((2, TILE + 8, W), F32),
        ],
        compiler_params=pltpu.CompilerParams(vmem_limit_bytes=56 * MIB),
        cost_estimate=pl.CostEstimate(
            flops=4_000_000_000, bytes_accessed=17_000_000, transcendentals=1_000_000
        ),
        name="query_part",
    )(x, halo, gain, qkv, conv, down, kf, rise, pos, b, scale)


def reading_kernel(m_ref, q_ref, u_ref, w_ref, z_ref, low_ref, up_ref, gain_ref, o_ref, r_ref, s_ref):
    n = m_ref.shape[0] // C
    ats = [pl.ds(c * C, C) for c in range(n)]
    ms = [m_ref[at, :] for at in ats]
    mu = [mm(ms[c], bd(u_ref[ats[c], :])) for c in range(n)]
    mw = [mm(ms[c], bd(w_ref[ats[c], :])) for c in range(n)]
    rd = [(q_ref[ats[c], :].astype(F32) - mw[c]).astype(BF16) for c in range(n)]
    for c in range(n):
        o_ref[ats[c], :] = (mu[c] + mm(rd[c], bd(z_ref[ats[c], : 2 * W]))).astype(BF16)
        r_ref[ats[c], :] = mm(rd[c], bd(z_ref[ats[c], 2 * W :])).astype(BF16)
    gate = mm(low_ref[...], up_ref[...])
    s_ref[...] = (
        gain_ref[...] * pl.reciprocal(1.0 + jnp.exp(-gate), approx=True)
    ).astype(BF16)


def reading_part(m, q, u, w, z, low, up, gain):
    tokens = m.shape[0]
    rank = low.shape[1]
    whole = lambda *shape: pl.BlockSpec(shape, lambda i: (0,) * len(shape))
    rows = lambda width: pl.BlockSpec((TILE, width), lambda i: (i, 0))
    return pl.pallas_call(
        reading_kernel,
        grid=(tokens // TILE,),
        in_specs=[rows(2 * W)] * 4
        + [rows(4 * W), rows(rank), whole(rank, 2 * W), whole(1, 2 * W)],
        out_specs=[rows(2 * W)] * 3,
        out_shape=[
            jax.ShapeDtypeStruct((tokens, 2 * W), BF16),
            jax.ShapeDtypeStruct((tokens, 2 * W), BF16),
            jax.ShapeDtypeStruct((tokens, 2 * W), BF16),
        ],
        compiler_params=pltpu.CompilerParams(vmem_limit_bytes=56 * MIB),
        cost_estimate=pl.CostEstimate(
            flops=3_000_000_000, bytes_accessed=12_000_000, transcendentals=1_000_000
        ),
        name="reading_part",
    )(m, q, u, w, z, low, up, gain)


def compose_kernel(zi_ref, own, one, two, three, tot_ref, pre_ref, slots):
    z = zi_ref[0]
    for d, ref in enumerate((own, one, two, three)):
        slots[d] = ref[...]
    rows = lax.broadcasted_iota(jnp.int32, (W, 2 * W), 0)
    cols = lax.broadcasted_iota(jnp.int32, (W, 2 * W), 1) % W
    first = slots[z]
    pb = jnp.zeros((W, 2 * W), F32)
    pa = (rows == cols).astype(F32)
    tb = first[:, : 2 * W].astype(F32)
    ta = first[:, 2 * W :].astype(F32)
    for j in range(1, 4):
        here = j == z
        pb = jnp.where(here, tb, pb)
        pa = jnp.where(here, ta, pa)
        nxt = slots[lax.rem(z - j + 4, 4)]
        a = nxt[:, 2 * W :]
        tb = nxt[:, : 2 * W].astype(F32) + mm(a, bd(tb.astype(BF16)))
        ta = mm(a, bd(ta.astype(BF16)))
    tot_ref[:, : 2 * W] = tb.astype(BF16)
    tot_ref[:, 2 * W :] = ta.astype(BF16)
    pre_ref[:, : 2 * W] = pb.astype(BF16)
    pre_ref[:, 2 * W :] = pa.astype(BF16)


def compose(zi, own, one, two, three):
    shape = jax.ShapeDtypeStruct(own.shape, BF16)
    return pl.pallas_call(
        compose_kernel,
        in_specs=[pl.BlockSpec(memory_space=pltpu.SMEM)]
        + [pl.BlockSpec(memory_space=pltpu.VMEM)] * 4,
        out_specs=[pl.BlockSpec(memory_space=pltpu.VMEM)] * 2,
        out_shape=[shape, shape],
        scratch_shapes=[pltpu.VMEM((4,) + own.shape, BF16)],
        compiler_params=pltpu.CompilerParams(vmem_limit_bytes=4 * MIB),
        cost_estimate=pl.CostEstimate(
            flops=30_000_000, bytes_accessed=800_000, transcendentals=0
        ),
        name="compose",
    )(zi, own, one, two, three)


def gated_kernel(at_ref, one, two, three, pre, o_hbm, r_hbm, s_hbm, *rest):
    outs, (o_ref, r_ref, s_ref, sems) = rest[:4], rest[4:]
    xi, yi = at_ref[0], at_ref[1]
    copies = [
        pltpu.make_async_copy(src, dst, sems.at[i])
        for i, (src, dst) in enumerate(((r_hbm, r_ref), (o_hbm, o_ref), (s_hbm, s_ref)))
    ]
    for copy in copies:
        copy.start()
    s = jnp.zeros((W, 2 * W), F32)
    for d, ref in ((3, three), (2, two), (1, one)):
        nxt = ref[:, : 2 * W].astype(F32) + mm(ref[:, 2 * W :], bd(s.astype(BF16)))
        s = jnp.where(xi >= d, nxt, s)
    s = pre[:, : 2 * W].astype(F32) + mm(pre[:, 2 * W :], bd(s.astype(BF16)))
    start = bd(s.astype(BF16))
    for copy in copies:
        copy.wait()
    for d, out in enumerate(outs):
        here = lax.rem(yi + d, 4)
        att = o_ref[here].astype(F32) + mm(r_ref[here], start)
        scale = per_head(
            att, lambda h: lax.rsqrt(jnp.mean(h * h, axis=-1, keepdims=True) + 1e-05)
        )
        out[...] = (att * scale * s_ref[here].astype(F32)).astype(BF16)


def gated_part(at, one, two, three, pre, o, r, s):
    part = o.shape[0] // 4
    vmem = pl.BlockSpec(memory_space=pltpu.VMEM)
    return pl.pallas_call(
        gated_kernel,
        in_specs=[pl.BlockSpec(memory_space=pltpu.SMEM)]
        + [vmem] * 4
        + [pl.BlockSpec(memory_space=pltpu.HBM)] * 3,
        out_specs=[vmem] * 4,
        out_shape=[jax.ShapeDtypeStruct((part, 2 * W), BF16)] * 4,
        scratch_shapes=[pltpu.VMEM((4, part, 2 * W), BF16)] * 3
        + [pltpu.SemaphoreType.DMA((3,))],
        compiler_params=pltpu.CompilerParams(vmem_limit_bytes=56 * MIB),
        cost_estimate=pl.CostEstimate(
            flops=300_000_000, bytes_accessed=4_000_000, transcendentals=10_000
        ),
        name="gated_part",
    )(at, one, two, three, pre, *(a.reshape(4, part, 2 * W) for a in (o, r, s)))


def turned_kernel(at_ref, w_ref, mine_ref, other_ref, held):
    features = w_ref.shape[1] // 8
    held[...] = w_ref[...].T
    for j in range(4):
        to = pl.ds(j * features, features)
        for ref, core in ((mine_ref, at_ref[1]), (other_ref, 1 - at_ref[1])):
            at = pl.multiple_of((2 * j + core) * features, 16)
            ref[to, :] = held[pl.ds(at, features), :]


def turned(at, w):
    k, n = w.shape
    half = jax.ShapeDtypeStruct((n // 2, k), w.dtype)
    return pl.pallas_call(
        turned_kernel,
        in_specs=[
            pl.BlockSpec(memory_space=pltpu.SMEM),
            pl.BlockSpec(memory_space=pltpu.VMEM),
        ],
        out_specs=[pl.BlockSpec(memory_space=pltpu.VMEM)] * 2,
        out_shape=[half, half],
        scratch_shapes=[pltpu.VMEM((n, k), w.dtype)],
        compiler_params=pltpu.CompilerParams(vmem_limit_bytes=8 * MIB),
        cost_estimate=pl.CostEstimate(
            flops=0, bytes_accessed=2_400_000, transcendentals=0
        ),
        name="turned",
    )(at, w)


def mixed_kernel(at_ref, *refs):
    del at_ref
    weights, blocks, outs = refs[:8], refs[8:16], refs[16:]
    total = None
    for w, g in zip(weights, blocks, strict=True):
        part = mm_nt(w[...], g[...])
        total = part if total is None else total + part
    total = total.astype(BF16)
    for i, out in enumerate(outs):

        @pl.when(pl.program_id(0) == i)
        def _():
            out[...] = total


def mixed_part(distances, at, weights, mine, theirs):
    features = weights[0][0].shape[0] // weights[0][2]
    tokens = mine[0].shape[0]
    first, step = distances[0], (distances[1] - distances[0] if len(distances) > 1 else 0)

    def wspec(base):
        return pl.BlockSpec(
            (features, 2 * W),
            lambda i, at: (base + lax.rem(at[0] + first + step * i, 4), 0),
        )

    gspec = pl.BlockSpec((tokens, 2 * W), lambda i, at: (0, 0))
    ospec = pl.BlockSpec((features, tokens), lambda i, at: (0, 0))
    return pl.pallas_call(
        mixed_kernel,
        grid_spec=pltpu.PrefetchScalarGridSpec(
            num_scalar_prefetch=1,
            grid=(len(distances),),
            in_specs=[wspec(base) for _, base, _ in weights] + [gspec] * 8,
            out_specs=[ospec] * len(distances),
        ),
        out_shape=[jax.ShapeDtypeStruct((features, tokens), BF16)] * len(distances),
        compiler_params=pltpu.CompilerParams(vmem_limit_bytes=16 * MIB),
        cost_estimate=pl.CostEstimate(
            flops=600_000_000 * len(distances),
            bytes_accessed=2_000_000 + 1_500_000 * len(distances),
            transcendentals=0,
        ),
        name="mixed_part",
    )(at, *(a for a, _, _ in weights), *mine, *theirs)


def joined_kernel(at_ref, *refs):
    out = refs[-1]
    tokens = refs[0].shape[1]
    for d, piece in enumerate(refs[:-1]):
        to = lax.rem(at_ref[0] - d + 4, 4) * tokens
        out[:, pl.ds(pl.multiple_of(to, tokens), tokens)] = piece[...]


def joined(at, pieces):
    features, tokens = pieces[0].shape
    vmem = pl.BlockSpec(memory_space=pltpu.VMEM)
    return pl.pallas_call(
        joined_kernel,
        in_specs=[pl.BlockSpec(memory_space=pltpu.SMEM)] + [vmem] * 4,
        out_specs=vmem,
        out_shape=jax.ShapeDtypeStruct((features, 4 * tokens), BF16),
        compiler_params=pltpu.CompilerParams(vmem_limit_bytes=10 * MIB),
        cost_estimate=pl.CostEstimate(
            flops=0, bytes_accessed=2_400_000, transcendentals=0
        ),
        name="joined",
    )(at, *pieces)


def body(
    activations,
    norm_gain,
    qkv_weight,
    conv_weight,
    gate_down_matrix,
    gate_up,
    log_forget_gates,
    step_size,
    out_gain,
    out_weight,
):
    tokens, d = activations.shape
    ctx = lax.axis_index("ctx")
    xi, zi = ctx // 4, ctx % 4
    head = lax.axis_index("head")
    yi, ci = head // 2, head % 2

    def along_y(a, by):
        return lax.ppermute(a, "head", [(i, (i + 2 * by) % 8) for i in range(8)])

    def across(a):
        return lax.ppermute(a, "head", [(i, i ^ 1) for i in range(8)])

    here = jnp.stack([yi, ci])
    mine, other = turned(here, out_weight)
    halo = lax.ppermute(
        activations[tokens - 16 :], "ctx", [(i, i + 1) for i in range(15)]
    )
    both = jnp.concatenate([mine, across(other)], axis=0)
    below, above = along_y(both, 1), along_y(both, 3)
    gain = norm_gain.reshape(d // W, W)
    scale, kf, rise, pos, u, w, z, fin = local_part(
        activations, halo, gain, qkv_weight, conv_weight, log_forget_gates, step_size
    )

    def along_z(a, by):
        pairs = [(4 * i + j, 4 * i + (j + by) % 4) for i in range(4) for j in range(4)]
        return lax.ppermute(a, "ctx", pairs)

    def along_x(a, by):
        pairs = [(4 * i + j, 4 * ((i + by) % 4) + j) for i in range(4) for j in range(4)]
        return lax.ppermute(a, "ctx", pairs)

    fin, below, above = lax.optimization_barrier((fin, below, above))
    half = both.shape[0] // 2
    far = along_y(above[:half], 3), along_y(below[half:], 1)
    z1, z3, z2 = along_z(fin, 1), along_z(fin, 3), along_z(fin, 2)
    low, m, q = query_part(
        activations,
        halo,
        gain,
        qkv_weight,
        conv_weight,
        gate_down_matrix,
        kf,
        rise,
        pos,
        step_size,
        scale,
    )
    o, r, s = reading_part(
        m, q, u, w, z, low, gate_up, out_gain.reshape(1, 2 * W)
    )
    total, before = compose(zi.reshape(1), fin, z1, z2, z3)
    x1, x3, x2 = along_x(total, 1), along_x(total, 3), along_x(total, 2)
    x1, far = lax.optimization_barrier((x1, far))
    at = jnp.stack([xi, yi])
    q0, q1, q2, q3 = gated_part(at, x1, x2, x3, before, o, r, s)
    own = [q0, along_y(q1, 1), along_y(q3, 3), along_y(q2, 2)]
    weights = [(both, 0, 8), (below, 0, 8), (above, 0, 8), (far[0], 0, 4)]
    weights += [(both, 4, 8), (below, 4, 8), (above, 4, 8), (far[1], 0, 4)]
    blocks = own, [across(a) for a in own]
    (p2,) = mixed_part((2,), here, weights, *blocks)
    here, p2 = lax.optimization_barrier((here, p2))
    p1, p3 = mixed_part((1, 3), here, weights, *blocks)
    here, p1 = lax.optimization_barrier((here, p1))
    (p0,) = mixed_part((0,), here, weights, *blocks)
    pieces = [p0, along_y(p1, 1), along_y(p2, 2), along_y(p3, 3)]
    return joined(yi.reshape(1), pieces).T


def solution(mesh):
    in_specs = (
        P("ctx", None),
        P(),
        P(None, None, "head"),
        P(None, None, "head"),
        P(),
        P(None, "head"),
        P("head", "ctx", None),
        P("head", "ctx"),
        P("head"),
        P("head", None),
    )
    out_specs = P("ctx", "head")
    return jax.shard_map(body, mesh=mesh, in_specs=in_specs, out_specs=out_specs, check_vma=False)
```

```python
import functools

import jax
import jax.numpy as jnp
from jax import lax
from jax.experimental import pallas as pl
from jax.experimental.pallas import tpu as pltpu
from jax.sharding import PartitionSpec as P

F32 = jnp.float32
BF16 = jnp.bfloat16
C = 128
W = 128
TILE = 512
MIB = 1024 * 1024


def mm(a, b):
    return jnp.dot(a, b, preferred_element_type=F32)


def mm_nt(a, b):
    return lax.dot_general(a, b, (((1,), (1,)), ((), ())), preferred_element_type=F32)


def bd(a):
    z = jnp.zeros((a.shape[0], W), a.dtype)
    return jnp.concatenate(
        [
            jnp.concatenate([a[:, :W], z], axis=1),
            jnp.concatenate([z, a[:, W:]], axis=1),
        ],
        axis=0,
    )


def per_head(a, fn):
    return jnp.concatenate(
        [
            jnp.broadcast_to(fn(a[:, :W]), (a.shape[0], W)),
            jnp.broadcast_to(fn(a[:, W:]), (a.shape[0], W)),
        ],
        axis=1,
    )


def local_kernel(
    x_ref,
    halo_ref,
    gain_ref,
    wk_ref,
    wv_ref,
    conv_ref,
    g_ref,
    b_ref,
    scale,
    kf_ref,
    rise_ref,
    pos_ref,
    u_ref,
    w_out_ref,
    z_ref,
    fin_ref,
    wide,
    fresh,
    proj,
    state,
):
    step = pl.program_id(0)
    tiles = pl.num_programs(0) - 1
    n = TILE // C
    chunks = range(n)

    def projecting():
        block = TILE // 4

        def product(i, r):
            at = pl.ds(r * block, block)
            p = mm(x_ref[at, :], wide[i])
            for h in range(2):
                fresh[i, h, at, :] = p[:, h * W : (h + 1) * W]

        def root(r):
            at = pl.ds(r * C, C)
            rows = x_ref[at, :].astype(F32)
            ms = jnp.mean(rows * rows, axis=-1, keepdims=True)
            scale[at, :] = jnp.broadcast_to(lax.rsqrt(ms + 1e-06), (C, W))

        def apply(r):
            at = pl.ds(r * C, C)
            to = pl.ds(8 + r * C, C)
            for i in range(2):
                for h in range(2):
                    proj[i, h, to, :] = fresh[i, h, at, :] * scale[at, :]

        products = [functools.partial(product, i, r) for i in range(2) for r in range(4)]
        roots = [functools.partial(root, r) for r in chunks]
        return products, roots, [functools.partial(apply, r) for r in chunks]

    def delta(products=(), roots=(), applies=()):
        products, roots = list(products), list(roots)

        def fill(parts, count=1):
            for part in parts[:count]:
                part()
            del parts[:count]

        rows = lax.broadcasted_iota(jnp.int32, (C, 2 * C), 0)
        cols = lax.broadcasted_iota(jnp.int32, (C, 2 * C), 1) % C
        strict = cols < rows
        inclusive = cols <= rows
        tri = inclusive.astype(F32).astype(BF16)
        taps = conv_ref[...].astype(F32)

        def conv(i, c):
            halves = []
            for h in range(2):
                total = None
                for j in range(4):
                    part = (
                        taps[i + 1, j : j + 1, h * W : (h + 1) * W]
                        * proj[i, h, pl.ds(5 + j + c * C, C), :]
                    )
                    total = part if total is None else total + part
                halves.append(total * pl.reciprocal(1.0 + jnp.exp(-total), approx=True))
            return halves

        def unit(halves, factor=1.0):
            return jnp.concatenate(
                [
                    h
                    * (lax.rsqrt(jnp.sum(h * h, axis=-1, keepdims=True) + 1e-06) * factor)
                    for h in halves
                ],
                axis=1,
            )

        beta, cum = [], []
        for c in chunks:
            at = pl.ds(c * C, C)
            beta.append(jnp.concatenate([b_ref[0:1, at], b_ref[1:2, at]], axis=1))
            g = jnp.concatenate([g_ref[0, at, :], g_ref[1, at, :]], axis=1)
            hi = g.astype(BF16)
            lo = (g - hi.astype(F32)).astype(BF16)
            cum.append(mm(tri, jnp.concatenate([hi, lo], axis=0)))
        k = []
        for c in chunks:
            k.append(unit(conv(0, c)))
        mid = [a[C // 2 - 1 : C // 2, :] for a in cum]
        last = [a[C - 1 : C, :] for a in cum]
        rise = [jnp.exp(cum[c] - mid[c]) for c in chunks]
        fall = [jnp.exp(mid[c] - cum[c]) for c in chunks]
        from_start = [jnp.exp(mid[c]) for c in chunks]
        to_end = [jnp.exp(last[c] - mid[c]) for c in chunks]
        kr = [k[c] * rise[c] for c in chunks]
        kf = [k[c] * fall[c] for c in chunks]
        v16 = [jnp.concatenate(conv(1, c), axis=1).astype(BF16) for c in chunks]
        kf16 = [a.astype(BF16) for a in kf]
        pairs = [mm_nt(kr[c].astype(BF16), bd(kf16[c])) for c in chunks]
        lower = [jnp.where(strict, pairs[c] * beta[c], 0.0) for c in chunks]
        for c in chunks:
            at = pl.ds(c * C, C)
            kf_ref[at, :] = kf16[c]
            rise_ref[at, :] = rise[c].astype(BF16)
            pos_ref[at, :] = (rise[c] * from_start[c]).astype(BF16)

        two = (rows // 2 == cols // 2) & strict
        eye = (rows == cols).astype(F32)
        inv = [(eye - jnp.where(two, lower[c], 0.0)).astype(BF16) for c in chunks]
        lower16 = [a.astype(BF16) for a in lower]
        size = 2
        while size < C:
            fill(roots)
            off = (
                (rows // (2 * size) == cols // (2 * size))
                & (rows % (2 * size) >= size)
                & (cols % (2 * size) < size)
            )
            keep = off.astype(F32).astype(BF16)
            left = [mm(lower16[c] * keep, bd(inv[c])).astype(BF16) for c in chunks]
            fill(products)
            both = [mm(inv[c], bd(left[c])).astype(BF16) for c in chunks]
            fill(products, 1)
            inv = [inv[c] - both[c] for c in chunks]
            size *= 2

        fill(products, len(products))
        fill(roots, len(roots))
        if applies:
            proj[:, :, 0:8, :] = proj[:, :, TILE : TILE + 8, :]
        for part in applies:
            part()
        kpos = [kr[c] * from_start[c] for c in chunks]
        u = [mm(inv[c], bd(v16[c])).astype(BF16) for c in chunks]
        w = [mm(inv[c], bd(kpos[c].astype(BF16))).astype(BF16) for c in chunks]
        kt = []
        for c in chunks:
            ke = kf[c] * to_end[c]
            both_t = jnp.concatenate([ke[:, :W].T, ke[:, W:].T], axis=1)
            kt.append((both_t * beta[c]).astype(BF16))
        bmat = [mm(kt[c], bd(u[c])) for c in chunks]
        emat = [mm(kt[c], bd(w[c])).astype(BF16) for c in chunks]
        ends = jnp.concatenate(
            [jnp.exp(last[c])[:, h * W : (h + 1) * W] for c in chunks for h in range(2)],
            axis=0,
        ).T
        zb = state[:, : 2 * W]
        za = state[:, 2 * W :]
        for c in chunks:
            at = pl.ds(c * C, C)
            u_ref[at, :] = u[c]
            w_out_ref[at, :] = w[c]
            zb16, za16 = zb.astype(BF16), za.astype(BF16)
            z_ref[at, : 2 * W] = zb16
            z_ref[at, 2 * W :] = za16
            decay = jnp.concatenate(
                [
                    jnp.broadcast_to(ends[:, 2 * c : 2 * c + 1], (W, W)),
                    jnp.broadcast_to(ends[:, 2 * c + 1 : 2 * c + 2], (W, W)),
                ],
                axis=1,
            )
            zb = decay * zb + bmat[c] - mm(emat[c], bd(zb16))
            za = decay * za - mm(emat[c], bd(za16))
        state[:, : 2 * W] = zb
        state[:, 2 * W :] = za

    @pl.when(step == 0)
    def _():
        gain = gain_ref[...].T
        for j in range(gain.shape[1]):
            at = pl.ds(j * W, W)
            column = gain[:, j : j + 1]
            for i, w_ref in enumerate((wk_ref, wv_ref)):
                wide[i, at, :] = (w_ref[0, at, :].astype(F32) * column).astype(BF16)
        rows = halo_ref[...].astype(F32)
        ms = jnp.mean(rows * rows, axis=-1, keepdims=True)
        for i in range(2):
            p = (mm(halo_ref[...], wide[i]) * lax.rsqrt(ms + 1e-06))[8:16]
            for h in range(2):
                proj[i, h, 0:8, :] = p[:, h * W : (h + 1) * W]
        rows = lax.broadcasted_iota(jnp.int32, (W, 2 * W), 0)
        cols = lax.broadcasted_iota(jnp.int32, (W, 2 * W), 1) % W
        state[:, : 2 * W] = jnp.zeros((W, 2 * W), F32)
        state[:, 2 * W :] = (rows == cols).astype(F32)
        for parts in projecting():
            for part in parts:
                part()

    @pl.when((step > 0) & (step < tiles))
    def _():
        delta(*projecting())

    @pl.when(step == tiles)
    def _():
        delta()
        fin_ref[...] = state[...].astype(BF16)


def local_part(x, halo, gain, qkv, conv, g, b):
    tokens, d = x.shape
    grid = tokens // TILE
    whole = lambda *shape: pl.BlockSpec(shape, lambda i: (0,) * len(shape))
    first = lambda i: jnp.minimum(i, grid - 1)
    then = lambda i: jnp.maximum(i - 1, 0)
    early = lambda width: pl.BlockSpec((TILE, width), lambda i: (first(i), 0))
    rows = lambda width: pl.BlockSpec((TILE, width), lambda i: (then(i), 0))
    return pl.pallas_call(
        local_kernel,
        grid=(grid + 1,),
        in_specs=[
            early(d),
            whole(16, d),
            whole(d // W, W),
            pl.BlockSpec((1, d, 2 * W), lambda i: (1, 0, 0)),
            pl.BlockSpec((1, d, 2 * W), lambda i: (2, 0, 0)),
            whole(3, 4, 2 * W),
            pl.BlockSpec((2, TILE, W), lambda i: (0, then(i), 0)),
            pl.BlockSpec((2, TILE), lambda i: (0, then(i))),
        ],
        out_specs=[early(W)] + [rows(2 * W)] * 5 + [rows(4 * W), whole(W, 4 * W)],
        out_shape=[
            jax.ShapeDtypeStruct((tokens, W), F32),
            jax.ShapeDtypeStruct((tokens, 2 * W), BF16),
            jax.ShapeDtypeStruct((tokens, 2 * W), BF16),
            jax.ShapeDtypeStruct((tokens, 2 * W), BF16),
            jax.ShapeDtypeStruct((tokens, 2 * W), BF16),
            jax.ShapeDtypeStruct((tokens, 2 * W), BF16),
            jax.ShapeDtypeStruct((tokens, 4 * W), BF16),
            jax.ShapeDtypeStruct((W, 4 * W), BF16),
        ],
        scratch_shapes=[
            pltpu.VMEM((2, d, 2 * W), BF16),
            pltpu.VMEM((2, 2, TILE, W), F32),
            pltpu.VMEM((2, 2, TILE + 8, W), F32),
            pltpu.VMEM((W, 4 * W), F32),
        ],
        compiler_params=pltpu.CompilerParams(vmem_limit_bytes=56 * MIB),
        cost_estimate=pl.CostEstimate(
            flops=14_000_000_000, bytes_accessed=24_000_000, transcendentals=6_000_000
        ),
        name="local_part",
    )(x, halo, gain, qkv, qkv, conv, g, b)


def query_kernel(
    x_ref,
    halo_ref,
    gain_ref,
    w_ref,
    conv_ref,
    down_ref,
    kf_ref,
    rise_ref,
    pos_ref,
    b_ref,
    scale_ref,
    low_ref,
    m_ref,
    q_ref,
    wide,
    narrow,
    raw,
    proj,
):
    step = pl.program_id(0)
    tiles = pl.num_programs(0) - 1
    n = TILE // C

    def root(rows):
        wide_rows = rows.astype(F32)
        return lax.rsqrt(jnp.mean(wide_rows * wide_rows, axis=-1, keepdims=True) + 1e-06)

    def products():
        def queries():
            raw[...] = mm(x_ref[...], wide[...])

        def lowered():
            low = mm(x_ref[...], narrow[...])
            low_ref[...] = (low * scale_ref[...]).astype(BF16)

        return [queries, lowered]

    def keep():
        for h in range(2):
            proj[h, 8:, :] = raw[:, h * W : (h + 1) * W] * scale_ref[...]

    def finish(parts):
        parts = list(parts)
        taps = conv_ref[0].astype(F32)
        rows = lax.broadcasted_iota(jnp.int32, (C, 2 * C), 0)
        cols = lax.broadcasted_iota(jnp.int32, (C, 2 * C), 1) % C
        inclusive = cols <= rows
        for c in range(n):
            if parts:
                parts.pop(0)()
            at = pl.ds(c * C, C)
            halves = []
            for h in range(2):
                total = None
                for j in range(4):
                    part = (
                        taps[j : j + 1, h * W : (h + 1) * W]
                        * proj[h, pl.ds(5 + j + c * C, C), :]
                    )
                    total = part if total is None else total + part
                f = total * pl.reciprocal(1.0 + jnp.exp(-total), approx=True)
                size = lax.rsqrt(jnp.sum(f * f, axis=-1, keepdims=True) + 1e-06)
                halves.append(f * (size * W**-0.5))
            query = jnp.concatenate(halves, axis=1)
            risen = (query * rise_ref[at, :].astype(F32)).astype(BF16)
            q_ref[at, :] = (query * pos_ref[at, :].astype(F32)).astype(BF16)
            beta = jnp.concatenate([b_ref[0:1, at], b_ref[1:2, at]], axis=1)
            pairs = mm_nt(risen, bd(kf_ref[at, :]))
            m_ref[at, :] = jnp.where(inclusive, pairs * beta, 0.0).astype(BF16)

    @pl.when(step == 0)
    def _():
        gain = gain_ref[...].T
        for j in range(gain.shape[1]):
            at = pl.ds(j * W, W)
            column = gain[:, j : j + 1]
            wide[at, :] = (w_ref[0, at, :].astype(F32) * column).astype(BF16)
            narrow[at, :] = (down_ref[at, :].astype(F32) * column).astype(BF16)
        p = (mm(halo_ref[...], wide[...]) * root(halo_ref[...]))[8:16]
        for h in range(2):
            proj[h, 0:8, :] = p[:, h * W : (h + 1) * W]
        for part in products():
            part()
        keep()

    @pl.when((step > 0) & (step < tiles))
    def _():
        finish(products())
        proj[:, 0:8, :] = proj[:, TILE : TILE + 8, :]
        keep()

    @pl.when(step == tiles)
    def _():
        finish([])


def query_part(x, halo, gain, qkv, conv, down, kf, rise, pos, b, scale):
    tokens, d = x.shape
    rank = down.shape[1]
    whole = lambda *shape: pl.BlockSpec(shape, lambda i: (0,) * len(shape))
    grid = tokens // TILE
    first = lambda i: jnp.minimum(i, grid - 1)
    then = lambda i: jnp.maximum(i - 1, 0)
    early = lambda width: pl.BlockSpec((TILE, width), lambda i: (first(i), 0))
    rows = lambda width: pl.BlockSpec((TILE, width), lambda i: (then(i), 0))
    return pl.pallas_call(
        query_kernel,
        grid=(grid + 1,),
        in_specs=[
            early(d),
            whole(16, d),
            whole(d // W, W),
            whole(1, d, 2 * W),
            whole(3, 4, 2 * W),
            whole(d, rank),
            rows(2 * W),
            rows(2 * W),
            rows(2 * W),
            pl.BlockSpec((2, TILE), lambda i: (0, then(i))),
            early(W),
        ],
        out_specs=[early(rank), rows(2 * W), rows(2 * W)],
        out_shape=[
            jax.ShapeDtypeStruct((tokens, rank), BF16),
            jax.ShapeDtypeStruct((tokens, 2 * W), BF16),
            jax.ShapeDtypeStruct((tokens, 2 * W), BF16),
        ],
        scratch_shapes=[
            pltpu.VMEM((d, 2 * W), BF16),
            pltpu.VMEM((d, rank), BF16),
            pltpu.VMEM((TILE, 2 * W), F32),
            pltpu.VMEM((2, TILE + 8, W), F32),
        ],
        compiler_params=pltpu.CompilerParams(vmem_limit_bytes=56 * MIB),
        cost_estimate=pl.CostEstimate(
            flops=4_000_000_000, bytes_accessed=17_000_000, transcendentals=1_000_000
        ),
        name="query_part",
    )(x, halo, gain, qkv, conv, down, kf, rise, pos, b, scale)


def reading_kernel(m_ref, q_ref, u_ref, w_ref, z_ref, low_ref, up_ref, gain_ref, o_ref, r_ref, s_ref):
    n = m_ref.shape[0] // C
    ats = [pl.ds(c * C, C) for c in range(n)]
    ms = [m_ref[at, :] for at in ats]
    mu = [mm(ms[c], bd(u_ref[ats[c], :])) for c in range(n)]
    mw = [mm(ms[c], bd(w_ref[ats[c], :])) for c in range(n)]
    rd = [(q_ref[ats[c], :].astype(F32) - mw[c]).astype(BF16) for c in range(n)]
    for c in range(n):
        o_ref[ats[c], :] = (mu[c] + mm(rd[c], bd(z_ref[ats[c], : 2 * W]))).astype(BF16)
        r_ref[ats[c], :] = mm(rd[c], bd(z_ref[ats[c], 2 * W :])).astype(BF16)
    gate = mm(low_ref[...], up_ref[...])
    s_ref[...] = (
        gain_ref[...] * pl.reciprocal(1.0 + jnp.exp(-gate), approx=True)
    ).astype(BF16)


def reading_part(m, q, u, w, z, low, up, gain):
    tokens = m.shape[0]
    rank = low.shape[1]
    whole = lambda *shape: pl.BlockSpec(shape, lambda i: (0,) * len(shape))
    rows = lambda width: pl.BlockSpec((2 * TILE, width), lambda i: (i, 0))
    return pl.pallas_call(
        reading_kernel,
        grid=(tokens // (2 * TILE),),
        in_specs=[rows(2 * W)] * 4
        + [rows(4 * W), rows(rank), whole(rank, 2 * W), whole(1, 2 * W)],
        out_specs=[rows(2 * W)] * 3,
        out_shape=[
            jax.ShapeDtypeStruct((tokens, 2 * W), BF16),
            jax.ShapeDtypeStruct((tokens, 2 * W), BF16),
            jax.ShapeDtypeStruct((tokens, 2 * W), BF16),
        ],
        compiler_params=pltpu.CompilerParams(vmem_limit_bytes=56 * MIB),
        cost_estimate=pl.CostEstimate(
            flops=3_000_000_000, bytes_accessed=12_000_000, transcendentals=1_000_000
        ),
        name="reading_part",
    )(m, q, u, w, z, low, up, gain)


def compose_kernel(zi_ref, own, one, two, three, tot_ref, pre_ref, slots):
    z = zi_ref[0]
    for d, ref in enumerate((own, one, two, three)):
        slots[d] = ref[...]
    rows = lax.broadcasted_iota(jnp.int32, (W, 2 * W), 0)
    cols = lax.broadcasted_iota(jnp.int32, (W, 2 * W), 1) % W
    first = slots[z]
    pb = jnp.zeros((W, 2 * W), F32)
    pa = (rows == cols).astype(F32)
    tb = first[:, : 2 * W].astype(F32)
    ta = first[:, 2 * W :].astype(F32)
    for j in range(1, 4):
        here = j == z
        pb = jnp.where(here, tb, pb)
        pa = jnp.where(here, ta, pa)
        nxt = slots[lax.rem(z - j + 4, 4)]
        a = nxt[:, 2 * W :]
        tb = nxt[:, : 2 * W].astype(F32) + mm(a, bd(tb.astype(BF16)))
        ta = mm(a, bd(ta.astype(BF16)))
    tot_ref[:, : 2 * W] = tb.astype(BF16)
    tot_ref[:, 2 * W :] = ta.astype(BF16)
    pre_ref[:, : 2 * W] = pb.astype(BF16)
    pre_ref[:, 2 * W :] = pa.astype(BF16)


def compose(zi, own, one, two, three):
    shape = jax.ShapeDtypeStruct(own.shape, BF16)
    return pl.pallas_call(
        compose_kernel,
        in_specs=[pl.BlockSpec(memory_space=pltpu.SMEM)]
        + [pl.BlockSpec(memory_space=pltpu.VMEM)] * 4,
        out_specs=[pl.BlockSpec(memory_space=pltpu.VMEM)] * 2,
        out_shape=[shape, shape],
        scratch_shapes=[pltpu.VMEM((4,) + own.shape, BF16)],
        compiler_params=pltpu.CompilerParams(vmem_limit_bytes=4 * MIB),
        cost_estimate=pl.CostEstimate(
            flops=30_000_000, bytes_accessed=800_000, transcendentals=0
        ),
        name="compose",
    )(zi, own, one, two, three)


def gated_kernel(at_ref, one, two, three, pre, o_hbm, r_hbm, s_hbm, *rest):
    outs, (o_ref, r_ref, s_ref, sems) = rest[:4], rest[4:]
    xi, yi = at_ref[0], at_ref[1]
    quarters = [lax.rem(yi + d, 4) for d in range(4)]
    copies = [
        [
            pltpu.make_async_copy(src.at[here], dst.at[d], sems.at[3 * d + i])
            for i, (src, dst) in enumerate(((r_hbm, r_ref), (o_hbm, o_ref), (s_hbm, s_ref)))
        ]
        for d, here in enumerate(quarters)
    ]
    for d in range(4):
        for copy in copies[d]:
            copy.start()
    s = jnp.zeros((W, 2 * W), F32)
    for d, ref in ((3, three), (2, two), (1, one)):
        nxt = ref[:, : 2 * W].astype(F32) + mm(ref[:, 2 * W :], bd(s.astype(BF16)))
        s = jnp.where(xi >= d, nxt, s)
    s = pre[:, : 2 * W].astype(F32) + mm(pre[:, 2 * W :], bd(s.astype(BF16)))
    start = bd(s.astype(BF16))
    for d, out in enumerate(outs):
        for copy in copies[d]:
            copy.wait()
        att = o_ref[d].astype(F32) + mm(r_ref[d], start)
        scale = per_head(
            att, lambda h: lax.rsqrt(jnp.mean(h * h, axis=-1, keepdims=True) + 1e-05)
        )
        out[...] = (att * scale * s_ref[d].astype(F32)).astype(BF16)


def gated_part(at, one, two, three, pre, o, r, s):
    part = o.shape[0] // 4
    vmem = pl.BlockSpec(memory_space=pltpu.VMEM)
    return pl.pallas_call(
        gated_kernel,
        in_specs=[pl.BlockSpec(memory_space=pltpu.SMEM)]
        + [vmem] * 4
        + [pl.BlockSpec(memory_space=pltpu.HBM)] * 3,
        out_specs=[vmem] * 4,
        out_shape=[jax.ShapeDtypeStruct((part, 2 * W), BF16)] * 4,
        scratch_shapes=[pltpu.VMEM((4, part, 2 * W), BF16)] * 3
        + [pltpu.SemaphoreType.DMA((12,))],
        compiler_params=pltpu.CompilerParams(vmem_limit_bytes=56 * MIB),
        cost_estimate=pl.CostEstimate(
            flops=300_000_000, bytes_accessed=4_000_000, transcendentals=10_000
        ),
        name="gated_part",
    )(at, one, two, three, pre, *(a.reshape(4, part, 2 * W) for a in (o, r, s)))


def turned_kernel(at_ref, w_ref, mine_ref, other_ref, held):
    features = w_ref.shape[1] // 8
    held[...] = w_ref[...].T
    for j in range(4):
        to = pl.ds(j * features, features)
        for ref, core in ((mine_ref, at_ref[1]), (other_ref, 1 - at_ref[1])):
            at = pl.multiple_of((2 * j + core) * features, 16)
            ref[to, :] = held[pl.ds(at, features), :]


def turned(at, w):
    k, n = w.shape
    half = jax.ShapeDtypeStruct((n // 2, k), w.dtype)
    return pl.pallas_call(
        turned_kernel,
        in_specs=[
            pl.BlockSpec(memory_space=pltpu.SMEM),
            pl.BlockSpec(memory_space=pltpu.VMEM),
        ],
        out_specs=[pl.BlockSpec(memory_space=pltpu.VMEM)] * 2,
        out_shape=[half, half],
        scratch_shapes=[pltpu.VMEM((n, k), w.dtype)],
        compiler_params=pltpu.CompilerParams(vmem_limit_bytes=8 * MIB),
        cost_estimate=pl.CostEstimate(
            flops=0, bytes_accessed=2_400_000, transcendentals=0
        ),
        name="turned",
    )(at, w)


def mixed_kernel(at_ref, *refs):
    del at_ref
    weights, blocks, outs = refs[:8], refs[8:16], refs[16:]
    total = None
    for w, g in zip(weights, blocks, strict=True):
        part = mm_nt(w[...], g[...])
        total = part if total is None else total + part
    total = total.astype(BF16)
    for i, out in enumerate(outs):

        @pl.when(pl.program_id(0) == i)
        def _():
            out[...] = total


def mixed_part(distances, at, weights, mine, theirs):
    features = weights[0][0].shape[0] // weights[0][2]
    tokens = mine[0].shape[0]
    first, step = distances[0], (distances[1] - distances[0] if len(distances) > 1 else 0)

    def wspec(base):
        return pl.BlockSpec(
            (features, 2 * W),
            lambda i, at: (base + lax.rem(at[0] + first + step * i, 4), 0),
        )

    gspec = pl.BlockSpec((tokens, 2 * W), lambda i, at: (0, 0))
    ospec = pl.BlockSpec((features, tokens), lambda i, at: (0, 0))
    return pl.pallas_call(
        mixed_kernel,
        grid_spec=pltpu.PrefetchScalarGridSpec(
            num_scalar_prefetch=1,
            grid=(len(distances),),
            in_specs=[wspec(base) for _, base, _ in weights] + [gspec] * 8,
            out_specs=[ospec] * len(distances),
        ),
        out_shape=[jax.ShapeDtypeStruct((features, tokens), BF16)] * len(distances),
        compiler_params=pltpu.CompilerParams(vmem_limit_bytes=16 * MIB),
        cost_estimate=pl.CostEstimate(
            flops=600_000_000 * len(distances),
            bytes_accessed=2_000_000 + 1_500_000 * len(distances),
            transcendentals=0,
        ),
        name="mixed_part",
    )(at, *(a for a, _, _ in weights), *mine, *theirs)


def joined_kernel(at_ref, *refs):
    out = refs[-1]
    tokens = refs[0].shape[1]
    for d, piece in enumerate(refs[:-1]):
        to = lax.rem(at_ref[0] - d + 4, 4) * tokens
        out[:, pl.ds(pl.multiple_of(to, tokens), tokens)] = piece[...]


def joined(at, pieces):
    features, tokens = pieces[0].shape
    vmem = pl.BlockSpec(memory_space=pltpu.VMEM)
    return pl.pallas_call(
        joined_kernel,
        in_specs=[pl.BlockSpec(memory_space=pltpu.SMEM)] + [vmem] * 4,
        out_specs=vmem,
        out_shape=jax.ShapeDtypeStruct((features, 4 * tokens), BF16),
        compiler_params=pltpu.CompilerParams(vmem_limit_bytes=10 * MIB),
        cost_estimate=pl.CostEstimate(
            flops=0, bytes_accessed=2_400_000, transcendentals=0
        ),
        name="joined",
    )(at, *pieces)


def body(
    activations,
    norm_gain,
    qkv_weight,
    conv_weight,
    gate_down_matrix,
    gate_up,
    log_forget_gates,
    step_size,
    out_gain,
    out_weight,
):
    tokens, d = activations.shape
    ctx = lax.axis_index("ctx")
    xi, zi = ctx // 4, ctx % 4
    head = lax.axis_index("head")
    yi, ci = head // 2, head % 2

    def along_y(a, by):
        return lax.ppermute(a, "head", [(i, (i + 2 * by) % 8) for i in range(8)])

    def across(a):
        return lax.ppermute(a, "head", [(i, i ^ 1) for i in range(8)])

    here = jnp.stack([yi, ci])
    mine, other = turned(here, out_weight)
    halo = lax.ppermute(
        activations[tokens - 16 :], "ctx", [(i, i + 1) for i in range(15)]
    )
    both = jnp.concatenate([mine, across(other)], axis=0)
    below, above = along_y(both, 1), along_y(both, 3)
    gain = norm_gain.reshape(d // W, W)
    scale, kf, rise, pos, u, w, z, fin = local_part(
        activations, halo, gain, qkv_weight, conv_weight, log_forget_gates, step_size
    )

    def along_z(a, by):
        pairs = [(4 * i + j, 4 * i + (j + by) % 4) for i in range(4) for j in range(4)]
        return lax.ppermute(a, "ctx", pairs)

    def along_x(a, by):
        pairs = [(4 * i + j, 4 * ((i + by) % 4) + j) for i in range(4) for j in range(4)]
        return lax.ppermute(a, "ctx", pairs)

    kf, below, above = lax.optimization_barrier((kf, below, above))
    half = both.shape[0] // 2
    far = along_y(above[:half], 3), along_y(below[half:], 1)
    z1, z3, z2 = along_z(fin, 1), along_z(fin, 3), along_z(fin, 2)
    low, m, q = query_part(
        activations,
        halo,
        gain,
        qkv_weight,
        conv_weight,
        gate_down_matrix,
        kf,
        rise,
        pos,
        step_size,
        scale,
    )
    z2, m = lax.optimization_barrier((z2, m))
    o, r, s = reading_part(
        m, q, u, w, z, low, gate_up, out_gain.reshape(1, 2 * W)
    )
    total, before = compose(zi.reshape(1), fin, z1, z2, z3)
    x1, x3, x2 = along_x(total, 1), along_x(total, 3), along_x(total, 2)
    x1, far = lax.optimization_barrier((x1, far))
    at = jnp.stack([xi, yi])
    q0, q1, q2, q3 = gated_part(at, x1, x2, x3, before, o, r, s)
    own = [q0, along_y(q1, 1), along_y(q3, 3), along_y(q2, 2)]
    weights = [(both, 0, 8), (below, 0, 8), (above, 0, 8), (far[0], 0, 4)]
    weights += [(both, 4, 8), (below, 4, 8), (above, 4, 8), (far[1], 0, 4)]
    blocks = own, [across(a) for a in own]
    (p2,) = mixed_part((2,), here, weights, *blocks)
    here, p2 = lax.optimization_barrier((here, p2))
    p1, p3 = mixed_part((1, 3), here, weights, *blocks)
    far_piece = along_y(p2, 2)
    here, far_piece = lax.optimization_barrier((here, far_piece))
    (p0,) = mixed_part((0,), here, weights, *blocks)
    pieces = [p0, along_y(p1, 1), far_piece, along_y(p3, 3)]
    return joined(yi.reshape(1), pieces).T


def solution(mesh):
    in_specs = (
        P("ctx", None),
        P(),
        P(None, None, "head"),
        P(None, None, "head"),
        P(),
        P(None, "head"),
        P("head", "ctx", None),
        P("head", "ctx"),
        P("head"),
        P("head", None),
    )
    out_specs = P("ctx", "head")
    return jax.shard_map(body, mesh=mesh, in_specs=in_specs, out_specs=out_specs, check_vma=False)
```

```python
import functools

import jax
import jax.numpy as jnp
from jax import lax
from jax.experimental import pallas as pl
from jax.experimental.pallas import tpu as pltpu
from jax.sharding import PartitionSpec as P

F32 = jnp.float32
BF16 = jnp.bfloat16
C = 128
W = 128
TILE = 512
MIB = 1024 * 1024


def mm(a, b):
    return jnp.dot(a, b, preferred_element_type=F32)


def mm_nt(a, b):
    return lax.dot_general(a, b, (((1,), (1,)), ((), ())), preferred_element_type=F32)


def bd(a):
    z = jnp.zeros((a.shape[0], W), a.dtype)
    return jnp.concatenate(
        [
            jnp.concatenate([a[:, :W], z], axis=1),
            jnp.concatenate([z, a[:, W:]], axis=1),
        ],
        axis=0,
    )


def per_head(a, fn):
    return jnp.concatenate(
        [
            jnp.broadcast_to(fn(a[:, :W]), (a.shape[0], W)),
            jnp.broadcast_to(fn(a[:, W:]), (a.shape[0], W)),
        ],
        axis=1,
    )


def local_kernel(
    x_ref,
    halo_ref,
    gain_ref,
    wk_ref,
    wv_ref,
    conv_ref,
    g_ref,
    b_ref,
    scale,
    kf_ref,
    rise_ref,
    pos_ref,
    u_ref,
    w_out_ref,
    z_ref,
    fin_ref,
    wide,
    fresh,
    proj,
    state,
):
    step = pl.program_id(0)
    tiles = pl.num_programs(0) - 1
    n = TILE // C
    chunks = range(n)

    def projecting():
        block = TILE // 4

        def product(i, r):
            at = pl.ds(r * block, block)
            p = mm(x_ref[at, :], wide[i])
            for h in range(2):
                fresh[i, h, at, :] = p[:, h * W : (h + 1) * W]

        def root(r):
            at = pl.ds(r * C, C)
            rows = x_ref[at, :].astype(F32)
            ms = jnp.mean(rows * rows, axis=-1, keepdims=True)
            scale[at, :] = jnp.broadcast_to(lax.rsqrt(ms + 1e-06), (C, W))

        def apply(r):
            at = pl.ds(r * C, C)
            to = pl.ds(8 + r * C, C)
            for i in range(2):
                for h in range(2):
                    proj[i, h, to, :] = fresh[i, h, at, :] * scale[at, :]

        products = [functools.partial(product, i, r) for i in range(2) for r in range(4)]
        roots = [functools.partial(root, r) for r in chunks]
        return products, roots, [functools.partial(apply, r) for r in chunks]

    def delta(products=(), roots=(), applies=()):
        products, roots = list(products), list(roots)

        def fill(parts, count=1):
            for part in parts[:count]:
                part()
            del parts[:count]

        rows = lax.broadcasted_iota(jnp.int32, (C, 2 * C), 0)
        cols = lax.broadcasted_iota(jnp.int32, (C, 2 * C), 1) % C
        strict = cols < rows
        inclusive = cols <= rows
        tri = inclusive.astype(F32).astype(BF16)
        taps = conv_ref[...].astype(F32)

        def conv(i, c):
            halves = []
            for h in range(2):
                total = None
                for j in range(4):
                    part = (
                        taps[i + 1, j : j + 1, h * W : (h + 1) * W]
                        * proj[i, h, pl.ds(5 + j + c * C, C), :]
                    )
                    total = part if total is None else total + part
                halves.append(total * pl.reciprocal(1.0 + jnp.exp(-total), approx=True))
            return halves

        def unit(halves, factor=1.0):
            return jnp.concatenate(
                [
                    h
                    * (lax.rsqrt(jnp.sum(h * h, axis=-1, keepdims=True) + 1e-06) * factor)
                    for h in halves
                ],
                axis=1,
            )

        beta, cum = [], []
        for c in chunks:
            at = pl.ds(c * C, C)
            beta.append(jnp.concatenate([b_ref[0:1, at], b_ref[1:2, at]], axis=1))
            g = jnp.concatenate([g_ref[0, at, :], g_ref[1, at, :]], axis=1)
            hi = g.astype(BF16)
            lo = (g - hi.astype(F32)).astype(BF16)
            cum.append(mm(tri, jnp.concatenate([hi, lo], axis=0)))
        k = []
        for c in chunks:
            k.append(unit(conv(0, c)))
        mid = [a[C // 2 - 1 : C // 2, :] for a in cum]
        last = [a[C - 1 : C, :] for a in cum]
        rise = [jnp.exp(cum[c] - mid[c]) for c in chunks]
        fall = [jnp.exp(mid[c] - cum[c]) for c in chunks]
        from_start = [jnp.exp(mid[c]) for c in chunks]
        to_end = [jnp.exp(last[c] - mid[c]) for c in chunks]
        kr = [k[c] * rise[c] for c in chunks]
        kf = [k[c] * fall[c] for c in chunks]
        v16 = [jnp.concatenate(conv(1, c), axis=1).astype(BF16) for c in chunks]
        kf16 = [a.astype(BF16) for a in kf]
        pairs = [mm_nt(kr[c].astype(BF16), bd(kf16[c])) for c in chunks]
        lower = [jnp.where(strict, pairs[c] * beta[c], 0.0) for c in chunks]
        for c in chunks:
            at = pl.ds(c * C, C)
            kf_ref[at, :] = kf16[c]
            rise_ref[at, :] = rise[c].astype(BF16)
            pos_ref[at, :] = (rise[c] * from_start[c]).astype(BF16)

        two = (rows // 2 == cols // 2) & strict
        eye = (rows == cols).astype(F32)
        inv = [(eye - jnp.where(two, lower[c], 0.0)).astype(BF16) for c in chunks]
        lower16 = [a.astype(BF16) for a in lower]
        size = 2
        while size < C:
            fill(roots)
            off = (
                (rows // (2 * size) == cols // (2 * size))
                & (rows % (2 * size) >= size)
                & (cols % (2 * size) < size)
            )
            keep = off.astype(F32).astype(BF16)
            left = [mm(lower16[c] * keep, bd(inv[c])).astype(BF16) for c in chunks]
            fill(products)
            both = [mm(inv[c], bd(left[c])).astype(BF16) for c in chunks]
            fill(products, 1)
            inv = [inv[c] - both[c] for c in chunks]
            size *= 2

        fill(products, len(products))
        fill(roots, len(roots))
        if applies:
            proj[:, :, 0:8, :] = proj[:, :, TILE : TILE + 8, :]
        for part in applies:
            part()
        kpos = [kr[c] * from_start[c] for c in chunks]
        u = [mm(inv[c], bd(v16[c])).astype(BF16) for c in chunks]
        w = [mm(inv[c], bd(kpos[c].astype(BF16))).astype(BF16) for c in chunks]
        kt = []
        for c in chunks:
            ke = kf[c] * to_end[c]
            both_t = jnp.concatenate([ke[:, :W].T, ke[:, W:].T], axis=1)
            kt.append((both_t * beta[c]).astype(BF16))
        bmat = [mm(kt[c], bd(u[c])) for c in chunks]
        emat = [mm(kt[c], bd(w[c])).astype(BF16) for c in chunks]
        ends = jnp.concatenate(
            [jnp.exp(last[c])[:, h * W : (h + 1) * W] for c in chunks for h in range(2)],
            axis=0,
        ).T
        zb = state[:, : 2 * W]
        za = state[:, 2 * W :]
        for c in chunks:
            at = pl.ds(c * C, C)
            u_ref[at, :] = u[c]
            w_out_ref[at, :] = w[c]
            zb16, za16 = zb.astype(BF16), za.astype(BF16)
            z_ref[at, : 2 * W] = zb16
            z_ref[at, 2 * W :] = za16
            decay = jnp.concatenate(
                [
                    jnp.broadcast_to(ends[:, 2 * c : 2 * c + 1], (W, W)),
                    jnp.broadcast_to(ends[:, 2 * c + 1 : 2 * c + 2], (W, W)),
                ],
                axis=1,
            )
            zb = decay * zb + bmat[c] - mm(emat[c], bd(zb16))
            za = decay * za - mm(emat[c], bd(za16))
        state[:, : 2 * W] = zb
        state[:, 2 * W :] = za

    @pl.when(step == 0)
    def _():
        gain = gain_ref[...].T
        for j in range(gain.shape[1]):
            at = pl.ds(j * W, W)
            column = gain[:, j : j + 1]
            for i, w_ref in enumerate((wk_ref, wv_ref)):
                wide[i, at, :] = (w_ref[0, at, :].astype(F32) * column).astype(BF16)
        rows = halo_ref[...].astype(F32)
        ms = jnp.mean(rows * rows, axis=-1, keepdims=True)
        for i in range(2):
            p = (mm(halo_ref[...], wide[i]) * lax.rsqrt(ms + 1e-06))[8:16]
            for h in range(2):
                proj[i, h, 0:8, :] = p[:, h * W : (h + 1) * W]
        rows = lax.broadcasted_iota(jnp.int32, (W, 2 * W), 0)
        cols = lax.broadcasted_iota(jnp.int32, (W, 2 * W), 1) % W
        state[:, : 2 * W] = jnp.zeros((W, 2 * W), F32)
        state[:, 2 * W :] = (rows == cols).astype(F32)
        for parts in projecting():
            for part in parts:
                part()

    @pl.when((step > 0) & (step < tiles))
    def _():
        delta(*projecting())

    @pl.when(step == tiles)
    def _():
        delta()
        fin_ref[...] = state[...].astype(BF16)


def local_part(x, halo, gain, qkv, conv, g, b):
    tokens, d = x.shape
    grid = tokens // TILE
    whole = lambda *shape: pl.BlockSpec(shape, lambda i: (0,) * len(shape))
    first = lambda i: jnp.minimum(i, grid - 1)
    then = lambda i: jnp.maximum(i - 1, 0)
    early = lambda width: pl.BlockSpec((TILE, width), lambda i: (first(i), 0))
    rows = lambda width: pl.BlockSpec((TILE, width), lambda i: (then(i), 0))
    return pl.pallas_call(
        local_kernel,
        grid=(grid + 1,),
        in_specs=[
            early(d),
            whole(16, d),
            whole(d // W, W),
            pl.BlockSpec((1, d, 2 * W), lambda i: (1, 0, 0)),
            pl.BlockSpec((1, d, 2 * W), lambda i: (2, 0, 0)),
            whole(3, 4, 2 * W),
            pl.BlockSpec((2, TILE, W), lambda i: (0, then(i), 0)),
            pl.BlockSpec((2, TILE), lambda i: (0, then(i))),
        ],
        out_specs=[early(W)] + [rows(2 * W)] * 5 + [rows(4 * W), whole(W, 4 * W)],
        out_shape=[
            jax.ShapeDtypeStruct((tokens, W), F32),
            jax.ShapeDtypeStruct((tokens, 2 * W), BF16),
            jax.ShapeDtypeStruct((tokens, 2 * W), BF16),
            jax.ShapeDtypeStruct((tokens, 2 * W), BF16),
            jax.ShapeDtypeStruct((tokens, 2 * W), BF16),
            jax.ShapeDtypeStruct((tokens, 2 * W), BF16),
            jax.ShapeDtypeStruct((tokens, 4 * W), BF16),
            jax.ShapeDtypeStruct((W, 4 * W), BF16),
        ],
        scratch_shapes=[
            pltpu.VMEM((2, d, 2 * W), BF16),
            pltpu.VMEM((2, 2, TILE, W), F32),
            pltpu.VMEM((2, 2, TILE + 8, W), F32),
            pltpu.VMEM((W, 4 * W), F32),
        ],
        compiler_params=pltpu.CompilerParams(vmem_limit_bytes=56 * MIB),
        cost_estimate=pl.CostEstimate(
            flops=14_000_000_000, bytes_accessed=24_000_000, transcendentals=6_000_000
        ),
        name="local_part",
    )(x, halo, gain, qkv, qkv, conv, g, b)


def query_kernel(
    x_ref,
    halo_ref,
    gain_ref,
    w_ref,
    conv_ref,
    down_ref,
    kf_ref,
    rise_ref,
    pos_ref,
    b_ref,
    scale_ref,
    low_ref,
    m_ref,
    q_ref,
    wide,
    narrow,
    raw,
    proj,
):
    step = pl.program_id(0)
    tiles = pl.num_programs(0) - 1
    n = TILE // C

    def root(rows):
        wide_rows = rows.astype(F32)
        return lax.rsqrt(jnp.mean(wide_rows * wide_rows, axis=-1, keepdims=True) + 1e-06)

    def products():
        def queries():
            raw[...] = mm(x_ref[...], wide[...])

        def lowered():
            low = mm(x_ref[...], narrow[...])
            low_ref[...] = (low * scale_ref[...]).astype(BF16)

        return [queries, lowered]

    def keep():
        for h in range(2):
            proj[h, 8:, :] = raw[:, h * W : (h + 1) * W] * scale_ref[...]

    def finish(parts):
        parts = list(parts)
        taps = conv_ref[0].astype(F32)
        rows = lax.broadcasted_iota(jnp.int32, (C, 2 * C), 0)
        cols = lax.broadcasted_iota(jnp.int32, (C, 2 * C), 1) % C
        inclusive = cols <= rows
        for c in range(n):
            if parts:
                parts.pop(0)()
            at = pl.ds(c * C, C)
            halves = []
            for h in range(2):
                total = None
                for j in range(4):
                    part = (
                        taps[j : j + 1, h * W : (h + 1) * W]
                        * proj[h, pl.ds(5 + j + c * C, C), :]
                    )
                    total = part if total is None else total + part
                f = total * pl.reciprocal(1.0 + jnp.exp(-total), approx=True)
                size = lax.rsqrt(jnp.sum(f * f, axis=-1, keepdims=True) + 1e-06)
                halves.append(f * (size * W**-0.5))
            query = jnp.concatenate(halves, axis=1)
            risen = (query * rise_ref[at, :].astype(F32)).astype(BF16)
            q_ref[at, :] = (query * pos_ref[at, :].astype(F32)).astype(BF16)
            beta = jnp.concatenate([b_ref[0:1, at], b_ref[1:2, at]], axis=1)
            pairs = mm_nt(risen, bd(kf_ref[at, :]))
            m_ref[at, :] = jnp.where(inclusive, pairs * beta, 0.0).astype(BF16)

    @pl.when(step == 0)
    def _():
        gain = gain_ref[...].T
        for j in range(gain.shape[1]):
            at = pl.ds(j * W, W)
            column = gain[:, j : j + 1]
            wide[at, :] = (w_ref[0, at, :].astype(F32) * column).astype(BF16)
            narrow[at, :] = (down_ref[at, :].astype(F32) * column).astype(BF16)
        p = (mm(halo_ref[...], wide[...]) * root(halo_ref[...]))[8:16]
        for h in range(2):
            proj[h, 0:8, :] = p[:, h * W : (h + 1) * W]
        for part in products():
            part()
        keep()

    @pl.when((step > 0) & (step < tiles))
    def _():
        finish(products())
        proj[:, 0:8, :] = proj[:, TILE : TILE + 8, :]
        keep()

    @pl.when(step == tiles)
    def _():
        finish([])


def query_part(x, halo, gain, qkv, conv, down, kf, rise, pos, b, scale):
    tokens, d = x.shape
    rank = down.shape[1]
    whole = lambda *shape: pl.BlockSpec(shape, lambda i: (0,) * len(shape))
    grid = tokens // TILE
    first = lambda i: jnp.minimum(i, grid - 1)
    then = lambda i: jnp.maximum(i - 1, 0)
    early = lambda width: pl.BlockSpec((TILE, width), lambda i: (first(i), 0))
    rows = lambda width: pl.BlockSpec((TILE, width), lambda i: (then(i), 0))
    return pl.pallas_call(
        query_kernel,
        grid=(grid + 1,),
        in_specs=[
            early(d),
            whole(16, d),
            whole(d // W, W),
            whole(1, d, 2 * W),
            whole(3, 4, 2 * W),
            whole(d, rank),
            rows(2 * W),
            rows(2 * W),
            rows(2 * W),
            pl.BlockSpec((2, TILE), lambda i: (0, then(i))),
            early(W),
        ],
        out_specs=[early(rank), rows(2 * W), rows(2 * W)],
        out_shape=[
            jax.ShapeDtypeStruct((tokens, rank), BF16),
            jax.ShapeDtypeStruct((tokens, 2 * W), BF16),
            jax.ShapeDtypeStruct((tokens, 2 * W), BF16),
        ],
        scratch_shapes=[
            pltpu.VMEM((d, 2 * W), BF16),
            pltpu.VMEM((d, rank), BF16),
            pltpu.VMEM((TILE, 2 * W), F32),
            pltpu.VMEM((2, TILE + 8, W), F32),
        ],
        compiler_params=pltpu.CompilerParams(vmem_limit_bytes=56 * MIB),
        cost_estimate=pl.CostEstimate(
            flops=4_000_000_000, bytes_accessed=17_000_000, transcendentals=1_000_000
        ),
        name="query_part",
    )(x, halo, gain, qkv, conv, down, kf, rise, pos, b, scale)


def reading_kernel(m_ref, q_ref, u_ref, w_ref, z_ref, low_ref, up_ref, gain_ref, o_ref, r_ref, s_ref):
    n = m_ref.shape[0] // C
    ats = [pl.ds(c * C, C) for c in range(n)]
    ms = [m_ref[at, :] for at in ats]
    mu = [mm(ms[c], bd(u_ref[ats[c], :])) for c in range(n)]
    mw = [mm(ms[c], bd(w_ref[ats[c], :])) for c in range(n)]
    rd = [(q_ref[ats[c], :].astype(F32) - mw[c]).astype(BF16) for c in range(n)]
    for c in range(n):
        o_ref[ats[c], :] = (mu[c] + mm(rd[c], bd(z_ref[ats[c], : 2 * W]))).astype(BF16)
        r_ref[ats[c], :] = mm(rd[c], bd(z_ref[ats[c], 2 * W :])).astype(BF16)
    gate = mm(low_ref[...], up_ref[...])
    s_ref[...] = (
        gain_ref[...] * pl.reciprocal(1.0 + jnp.exp(-gate), approx=True)
    ).astype(BF16)


def reading_part(m, q, u, w, z, low, up, gain):
    tokens = m.shape[0]
    rank = low.shape[1]
    whole = lambda *shape: pl.BlockSpec(shape, lambda i: (0,) * len(shape))
    rows = lambda width: pl.BlockSpec((2 * TILE, width), lambda i: (i, 0))
    return pl.pallas_call(
        reading_kernel,
        grid=(tokens // (2 * TILE),),
        in_specs=[rows(2 * W)] * 4
        + [rows(4 * W), rows(rank), whole(rank, 2 * W), whole(1, 2 * W)],
        out_specs=[rows(2 * W)] * 3,
        out_shape=[
            jax.ShapeDtypeStruct((tokens, 2 * W), BF16),
            jax.ShapeDtypeStruct((tokens, 2 * W), BF16),
            jax.ShapeDtypeStruct((tokens, 2 * W), BF16),
        ],
        compiler_params=pltpu.CompilerParams(vmem_limit_bytes=56 * MIB),
        cost_estimate=pl.CostEstimate(
            flops=3_000_000_000, bytes_accessed=12_000_000, transcendentals=1_000_000
        ),
        name="reading_part",
    )(m, q, u, w, z, low, up, gain)


def compose_kernel(zi_ref, own, one, two, three, tot_ref, pre_ref, slots):
    z = zi_ref[0]
    for d, ref in enumerate((own, one, two, three)):
        slots[d] = ref[...]
    rows = lax.broadcasted_iota(jnp.int32, (W, 2 * W), 0)
    cols = lax.broadcasted_iota(jnp.int32, (W, 2 * W), 1) % W
    first = slots[z]
    pb = jnp.zeros((W, 2 * W), F32)
    pa = (rows == cols).astype(F32)
    tb = first[:, : 2 * W].astype(F32)
    ta = first[:, 2 * W :].astype(F32)
    for j in range(1, 4):
        here = j == z
        pb = jnp.where(here, tb, pb)
        pa = jnp.where(here, ta, pa)
        nxt = slots[lax.rem(z - j + 4, 4)]
        a = nxt[:, 2 * W :]
        tb = nxt[:, : 2 * W].astype(F32) + mm(a, bd(tb.astype(BF16)))
        ta = mm(a, bd(ta.astype(BF16)))
    tot_ref[:, : 2 * W] = tb.astype(BF16)
    tot_ref[:, 2 * W :] = ta.astype(BF16)
    pre_ref[:, : 2 * W] = pb.astype(BF16)
    pre_ref[:, 2 * W :] = pa.astype(BF16)


def compose(zi, own, one, two, three):
    shape = jax.ShapeDtypeStruct(own.shape, BF16)
    return pl.pallas_call(
        compose_kernel,
        in_specs=[pl.BlockSpec(memory_space=pltpu.SMEM)]
        + [pl.BlockSpec(memory_space=pltpu.VMEM)] * 4,
        out_specs=[pl.BlockSpec(memory_space=pltpu.VMEM)] * 2,
        out_shape=[shape, shape],
        scratch_shapes=[pltpu.VMEM((4,) + own.shape, BF16)],
        compiler_params=pltpu.CompilerParams(vmem_limit_bytes=4 * MIB),
        cost_estimate=pl.CostEstimate(
            flops=30_000_000, bytes_accessed=800_000, transcendentals=0
        ),
        name="compose",
    )(zi, own, one, two, three)


def gated_kernel(at_ref, one, two, three, pre, o_hbm, r_hbm, s_hbm, *rest):
    outs, (o_ref, r_ref, s_ref, sems) = rest[:4], rest[4:]
    xi, yi = at_ref[0], at_ref[1]
    quarters = [lax.rem(yi + d, 4) for d in range(4)]
    copies = [
        [
            pltpu.make_async_copy(src.at[here], dst.at[d], sems.at[3 * d + i])
            for i, (src, dst) in enumerate(((r_hbm, r_ref), (o_hbm, o_ref), (s_hbm, s_ref)))
        ]
        for d, here in enumerate(quarters)
    ]
    for d in range(4):
        for copy in copies[d]:
            copy.start()
    s = jnp.zeros((W, 2 * W), F32)
    for d, ref in ((3, three), (2, two), (1, one)):
        nxt = ref[:, : 2 * W].astype(F32) + mm(ref[:, 2 * W :], bd(s.astype(BF16)))
        s = jnp.where(xi >= d, nxt, s)
    s = pre[:, : 2 * W].astype(F32) + mm(pre[:, 2 * W :], bd(s.astype(BF16)))
    start = bd(s.astype(BF16))
    for d, out in enumerate(outs):
        for copy in copies[d]:
            copy.wait()
        att = o_ref[d].astype(F32) + mm(r_ref[d], start)
        scale = per_head(
            att, lambda h: lax.rsqrt(jnp.mean(h * h, axis=-1, keepdims=True) + 1e-05)
        )
        out[...] = (att * scale * s_ref[d].astype(F32)).astype(BF16)


def gated_part(at, one, two, three, pre, o, r, s):
    part = o.shape[0] // 4
    vmem = pl.BlockSpec(memory_space=pltpu.VMEM)
    return pl.pallas_call(
        gated_kernel,
        in_specs=[pl.BlockSpec(memory_space=pltpu.SMEM)]
        + [vmem] * 4
        + [pl.BlockSpec(memory_space=pltpu.HBM)] * 3,
        out_specs=[vmem] * 4,
        out_shape=[jax.ShapeDtypeStruct((part, 2 * W), BF16)] * 4,
        scratch_shapes=[pltpu.VMEM((4, part, 2 * W), BF16)] * 3
        + [pltpu.SemaphoreType.DMA((12,))],
        compiler_params=pltpu.CompilerParams(vmem_limit_bytes=56 * MIB),
        cost_estimate=pl.CostEstimate(
            flops=300_000_000, bytes_accessed=4_000_000, transcendentals=10_000
        ),
        name="gated_part",
    )(at, one, two, three, pre, *(a.reshape(4, part, 2 * W) for a in (o, r, s)))


def turned_kernel(at_ref, w_ref, mine_ref, other_ref, held):
    features = w_ref.shape[1] // 8
    held[...] = w_ref[...].T
    for j in range(4):
        to = pl.ds(j * features, features)
        for ref, core in ((mine_ref, at_ref[1]), (other_ref, 1 - at_ref[1])):
            at = pl.multiple_of((2 * j + core) * features, 16)
            ref[to, :] = held[pl.ds(at, features), :]


def turned(at, w):
    k, n = w.shape
    half = jax.ShapeDtypeStruct((n // 2, k), w.dtype)
    return pl.pallas_call(
        turned_kernel,
        in_specs=[
            pl.BlockSpec(memory_space=pltpu.SMEM),
            pl.BlockSpec(memory_space=pltpu.VMEM),
        ],
        out_specs=[pl.BlockSpec(memory_space=pltpu.VMEM)] * 2,
        out_shape=[half, half],
        scratch_shapes=[pltpu.VMEM((n, k), w.dtype)],
        compiler_params=pltpu.CompilerParams(vmem_limit_bytes=8 * MIB),
        cost_estimate=pl.CostEstimate(
            flops=0, bytes_accessed=2_400_000, transcendentals=0
        ),
        name="turned",
    )(at, w)


def mixed_kernel(at_ref, *refs):
    del at_ref
    weights, blocks, outs = refs[:8], refs[8:16], refs[16:]
    total = None
    for w, g in zip(weights, blocks, strict=True):
        part = mm_nt(w[...], g[...])
        total = part if total is None else total + part
    total = total.astype(BF16)
    for i, out in enumerate(outs):

        @pl.when(pl.program_id(0) == i)
        def _():
            out[...] = total


def mixed_part(distances, at, weights, mine, theirs):
    features = weights[0][0].shape[0] // weights[0][2]
    tokens = mine[0].shape[0]
    first, step = distances[0], (distances[1] - distances[0] if len(distances) > 1 else 0)

    def wspec(base):
        return pl.BlockSpec(
            (features, 2 * W),
            lambda i, at: (base + lax.rem(at[0] + first + step * i, 4), 0),
        )

    gspec = pl.BlockSpec((tokens, 2 * W), lambda i, at: (0, 0))
    ospec = pl.BlockSpec((features, tokens), lambda i, at: (0, 0))
    return pl.pallas_call(
        mixed_kernel,
        grid_spec=pltpu.PrefetchScalarGridSpec(
            num_scalar_prefetch=1,
            grid=(len(distances),),
            in_specs=[wspec(base) for _, base, _ in weights] + [gspec] * 8,
            out_specs=[ospec] * len(distances),
        ),
        out_shape=[jax.ShapeDtypeStruct((features, tokens), BF16)] * len(distances),
        compiler_params=pltpu.CompilerParams(vmem_limit_bytes=16 * MIB),
        cost_estimate=pl.CostEstimate(
            flops=600_000_000 * len(distances),
            bytes_accessed=2_000_000 + 1_500_000 * len(distances),
            transcendentals=0,
        ),
        name="mixed_part",
    )(at, *(a for a, _, _ in weights), *mine, *theirs)


def joined_kernel(at_ref, *refs):
    out = refs[-1]
    tokens = refs[0].shape[1]
    for d, piece in enumerate(refs[:-1]):
        to = lax.rem(at_ref[0] - d + 4, 4) * tokens
        out[:, pl.ds(pl.multiple_of(to, tokens), tokens)] = piece[...]


def joined(at, pieces):
    features, tokens = pieces[0].shape
    vmem = pl.BlockSpec(memory_space=pltpu.VMEM)
    return pl.pallas_call(
        joined_kernel,
        in_specs=[pl.BlockSpec(memory_space=pltpu.SMEM)] + [vmem] * 4,
        out_specs=vmem,
        out_shape=jax.ShapeDtypeStruct((features, 4 * tokens), BF16),
        compiler_params=pltpu.CompilerParams(vmem_limit_bytes=10 * MIB),
        cost_estimate=pl.CostEstimate(
            flops=0, bytes_accessed=2_400_000, transcendentals=0
        ),
        name="joined",
    )(at, *pieces)


def body(
    activations,
    norm_gain,
    qkv_weight,
    conv_weight,
    gate_down_matrix,
    gate_up,
    log_forget_gates,
    step_size,
    out_gain,
    out_weight,
):
    tokens, d = activations.shape
    ctx = lax.axis_index("ctx")
    xi, zi = ctx // 4, ctx % 4
    head = lax.axis_index("head")
    yi, ci = head // 2, head % 2

    def along_y(a, by):
        return lax.ppermute(a, "head", [(i, (i + 2 * by) % 8) for i in range(8)])

    def across(a):
        return lax.ppermute(a, "head", [(i, i ^ 1) for i in range(8)])

    here = jnp.stack([yi, ci])
    mine, other = turned(here, out_weight)
    halo = lax.ppermute(
        activations[tokens - 16 :], "ctx", [(i, i + 1) for i in range(15)]
    )
    both = jnp.concatenate([mine, across(other)], axis=0)
    below, above = along_y(both, 1), along_y(both, 3)
    gain = norm_gain.reshape(d // W, W)
    scale, kf, rise, pos, u, w, z, fin = local_part(
        activations, halo, gain, qkv_weight, conv_weight, log_forget_gates, step_size
    )

    def along_z(a, by):
        pairs = [(4 * i + j, 4 * i + (j + by) % 4) for i in range(4) for j in range(4)]
        return lax.ppermute(a, "ctx", pairs)

    def along_x(a, by):
        pairs = [(4 * i + j, 4 * ((i + by) % 4) + j) for i in range(4) for j in range(4)]
        return lax.ppermute(a, "ctx", pairs)

    kf, below, above = lax.optimization_barrier((kf, below, above))
    half = both.shape[0] // 2
    far = along_y(above[:half], 3), along_y(below[half:], 1)
    z1, z3, z2 = along_z(fin, 1), along_z(fin, 3), along_z(fin, 2)
    low, m, q = query_part(
        activations,
        halo,
        gain,
        qkv_weight,
        conv_weight,
        gate_down_matrix,
        kf,
        rise,
        pos,
        step_size,
        scale,
    )
    z2, m = lax.optimization_barrier((z2, m))
    o, r, s = reading_part(
        m, q, u, w, z, low, gate_up, out_gain.reshape(1, 2 * W)
    )
    total, before = compose(zi.reshape(1), fin, z1, z2, z3)
    x1, x3, x2 = along_x(total, 1), along_x(total, 3), along_x(total, 2)
    x1, far = lax.optimization_barrier((x1, far))
    at = jnp.stack([xi, yi])
    q0, q1, q2, q3 = gated_part(at, x1, x2, x3, before, o, r, s)
    opposite = along_y(q2, 2)
    own = [q0, along_y(q1, 1), along_y(q3, 3), opposite]
    weights = [(both, 0, 8), (below, 0, 8), (above, 0, 8), (far[0], 0, 4)]
    weights += [(both, 4, 8), (below, 4, 8), (above, 4, 8), (far[1], 0, 4)]
    blocks = own, [across(a) for a in own]
    (p2,) = mixed_part((2,), here, weights, *blocks)
    here, p2 = lax.optimization_barrier((here, p2))
    p1, p3 = mixed_part((1, 3), here, weights, *blocks)
    far_piece = along_y(p2, 2)
    here, far_piece = lax.optimization_barrier((here, far_piece))
    (p0,) = mixed_part((0,), here, weights, *blocks)
    pieces = [p0, along_y(p1, 1), far_piece, along_y(p3, 3)]
    return joined(yi.reshape(1), pieces).T


def solution(mesh):
    in_specs = (
        P("ctx", None),
        P(),
        P(None, None, "head"),
        P(None, None, "head"),
        P(),
        P(None, "head"),
        P("head", "ctx", None),
        P("head", "ctx"),
        P("head"),
        P("head", None),
    )
    out_specs = P("ctx", "head")
    return jax.shard_map(body, mesh=mesh, in_specs=in_specs, out_specs=out_specs, check_vma=False)
```
